512 devices in a mesh: tm: 8 (over z), gx: 8 (over x, core), gy: 8 (over y).
Axes of the slice: x: 4, y: 8, z: 8, core: 2. Of those that a mesh axis runs over, the one named last changes fastest.
Arguments:
- initial: float32 [64, 64, 1024], P(None, 'gx', 'gy'), may hold values from -6 to 6
- capacity: float32 [64, 64, 1024], P(None, 'gx', 'gy'), may hold values from 0.25 to 4
- profile: float32 [64], replicated, may hold values from 0.5 to 1.5
- bore_loop: int32 [64, 1024], P('gx', 'gy'), may hold values from 0 to 31, as said below
- plan: int32 [8, 2, 16], P('tm'), may hold values from 0 to 7
Outputs:
- states: float32 [8, 64, 64, 1024], P('tm', None, 'gx', 'gy')
The draws below stay inside these ranges and needn't reach their ends.
Inputs may be any that keep to these rules, and one draw needn't show every extreme that they name: `bore_loop`: a column holds a borehole of circuit v when v < 16; values of 16 or more mark columns without a borehole; all boreholes lie in one lateral rectangle of 16 to 32 rows and 256 to 512 columns, placed anywhere.
All inputs are finite; a program needn't handle non-finite values.
Results may differ from the reference program's by a relative error of at most 0.0001.
Values sent between devices are 32-bit elements; how exact they have to be, the bound alone decides.
A program may use at most 64 MiB of HBM per device.

```python
import math
from functools import partial
import jax
import jax.numpy as jnp
import numpy as np
from jax import lax

NZ = 64
STEPS = 2
ITERS = 3
TERMS = 8
LOOPS = 16
SLICES = 8
SECTIONS = 3
NX = 64
NY = 1024


def lateral_level(key, swing_rows, swing_cols, offset):
    keys = jax.random.split(key, 2)
    row_phase = jax.random.uniform(keys[0], (), jnp.float32, 0.0, 1.0)
    col_phase = jax.random.uniform(keys[1], (), jnp.float32, 0.0, 1.0)
    rows = lax.broadcasted_iota(jnp.float32, (1, NX, NY), 1) / NX
    cols = lax.broadcasted_iota(jnp.float32, (1, NX, NY), 2) / NY
    row_wave = jnp.sin(2.0 * jnp.pi * (1.5 * rows + row_phase))
    col_wave = jnp.sin(2.0 * jnp.pi * (cols + col_phase))
    return jnp.exp(swing_rows * row_wave + swing_cols * col_wave + offset)


def draw_initial(key, part):
    key = jax.random.fold_in(key, 5)
    keys = jax.random.split(key, 2)
    level = lateral_level(keys[0], 1.3, 0.5, -0.6)
    values = jax.random.normal(keys[1], (NZ, NX, NY), jnp.float32) * level
    return jnp.clip(values, -6.0, 6.0).astype(jnp.float32)


def draw_bore_loop(key, part):
    key = jax.random.fold_in(key, 11)
    keys = jax.random.split(key, 6)
    height = jax.random.randint(keys[0], (), NX // 4, NX // 2 + 1)
    width = jax.random.randint(keys[1], (), NY // 4, NY // 2 + 1)
    row_start = jax.random.randint(keys[2], (), 0, NX - height + 1)
    col_start = jax.random.randint(keys[3], (), 0, NY - width + 1)
    rows = lax.broadcasted_iota(jnp.int32, (NX, NY), 0)
    cols = lax.broadcasted_iota(jnp.int32, (NX, NY), 1)
    inside = (rows >= row_start) & (rows < row_start + height) & (cols >= col_start) & (cols < col_start + width)
    field_ids = jax.random.randint(keys[4], (NX, NY), 0, LOOPS + LOOPS // 2)
    empty_ids = jax.random.randint(keys[5], (NX, NY), LOOPS, 2 * LOOPS)
    return jnp.where(inside, field_ids, empty_ids).astype(jnp.int32)


def plant(values, stream_key, smallest, top_value):
    shape = values.shape
    spot = [jax.random.randint(jax.random.fold_in(stream_key, axis), (), 0, shape[axis]) for axis in range(len(shape))]
    values = values.at[tuple(spot)].set(smallest)
    longest = shape.index(max(shape))
    spot[longest] = (spot[longest] + 1) % shape[longest]
    return values.at[tuple(spot)].set(top_value)


def block_scale(stream_key, shape, cuts, least, high):
    factor_of, own = 1.0, jax.random.fold_in(stream_key, 6)
    for axis_at, shards_of in cuts:
        steps = jnp.exp(jax.random.uniform(jax.random.fold_in(own, axis_at), (shards_of,), jnp.float32, least / len(cuts), high / len(cuts)))
        factor_of = factor_of * jnp.repeat(steps, shape[axis_at] // shards_of).reshape([-1 if axis == axis_at else 1 for axis in range(len(shape))])
    return factor_of


def setup_inputs(seed: int = 0) -> dict:
    key_of = jax.random.split(jax.random.key(seed), 6)
    return {
        "initial": draw_initial(jax.random.fold_in(key_of[5], 71), 0),
        "capacity": jnp.clip(jnp.exp(math.log(4.0) - 2.7725887 * jax.random.uniform(key_of[1], (NZ, NX, NY), jnp.float32) ** block_scale(key_of[1], (NZ, NX, NY), ((1, 8), (2, 8)), -0.2, 0.2)), 0.25, 4.0),
        "profile": jnp.clip(jax.random.uniform(key_of[2], (NZ,), jnp.float32, 0.5, 1.5), 0.5, 1.5),
        "bore_loop": draw_bore_loop(jax.random.fold_in(key_of[5], 71), 0),
        "plan": plant(jax.random.randint(key_of[4], (SLICES, STEPS, LOOPS), 0, 8), jax.random.fold_in(key_of[4], 1), 0, 7).astype(jnp.int32),
    }


HORIZON = 4.0 / 3.0
EXPONENT = 16.0


def cheb_coeffs(term_count):
    angles = np.pi * (np.arange(term_count) + 0.5) / term_count
    cheb_nodes = np.cos(angles)
    samples = np.exp(-EXPONENT * (cheb_nodes + 1.0))
    coeffs = [2.0 / term_count * float(np.sum(samples * np.cos(term_index * angles))) for term_index in range(term_count)]
    coeffs[0] = coeffs[0] / 2.0
    return coeffs


def stiffness(vector):
    padded = jnp.pad(vector, 1)
    beside_all = padded[2:, 1:-1, 1:-1] + padded[:-2, 1:-1, 1:-1]
    beside_all = beside_all + padded[1:-1, 2:, 1:-1] + padded[1:-1, :-2, 1:-1]
    beside_all = beside_all + padded[1:-1, 1:-1, 2:] + padded[1:-1, 1:-1, :-2]
    return 6.0 * vector - beside_all


def chebyshev(start_vec, apply_shifted, coeffs):
    previous = start_vec
    current = apply_shifted(start_vec)
    accumulated = coeffs[0] * previous + coeffs[1] * current
    for term_index in range(2, len(coeffs)):
        following = 2.0 * apply_shifted(current) - previous
        accumulated = accumulated + coeffs[term_index] * following
        previous, current = current, following
    return accumulated


def shifted_local(vector, inverse_cap, span_scale):
    return span_scale * stiffness(vector) * inverse_cap - vector


def solve_slice(start_vec, capacity, profile, bore_loop, slice_table, slice_length):
    time_step = slice_length / STEPS
    mass_term = capacity / time_step
    diagonal = mass_term + 6.0
    loop_ids = jnp.arange(LOOPS, dtype=jnp.int32)
    matches = bore_loop.astype(jnp.int32)[None, :, :] == loop_ids[:, None, None]
    current_state = start_vec
    for step_index in range(STEPS):
        rate_table = slice_table[step_index].astype(jnp.float32) - 3.5
        column = jnp.sum(jnp.where(matches, rate_table[:, None, None], jnp.float32(0.0)), axis=0)
        right_side = mass_term * current_state + profile[:, None, None] * column[None, :, :]
        solution = current_state
        residual = right_side - (mass_term * solution + stiffness(solution))
        precond = residual / diagonal
        inner_now = jnp.sum(residual * precond)
        direction = precond
        for iteration in range(ITERS):
            applied = mass_term * direction + stiffness(direction)
            step_size = inner_now / jnp.sum(direction * applied)
            solution = solution + step_size * direction
            residual = residual - step_size * applied
            if iteration + 1 < ITERS:
                precond = residual / diagonal
                inner_next = jnp.sum(residual * precond)
                direction = precond + (inner_next / inner_now) * direction
                inner_now = inner_next
        current_state = solution
    return current_state


def reference(initial, capacity, profile, bore_loop, plan):
    slice_length = HORIZON / SLICES
    inverse_cap = 1.0 / capacity
    slice_ends = []
    for slice_index in range(SLICES):
        start_vec = initial if slice_index == 0 else jnp.zeros_like(initial)
        slice_ends.append(solve_slice(start_vec, capacity, profile, bore_loop, plan[slice_index], slice_length))
    states = jnp.stack(slice_ends)
    coeffs = cheb_coeffs(TERMS)
    for section_index in range(SECTIONS):
        span_count = 2 ** section_index
        span_scale = span_count / (12.0 * SLICES)
        apply_shifted = partial(shifted_local, inverse_cap=inverse_cap, span_scale=span_scale)
        moved_states = [chebyshev(states[slice_index], apply_shifted, coeffs) for slice_index in range(SLICES - span_count)]
        states = states + jnp.concatenate([jnp.zeros_like(states[:span_count]), jnp.stack(moved_states)], axis=0)
    return states
```

```python
import functools

import jax
import jax.numpy as jnp
import numpy as np
from jax import lax
from jax.experimental import pallas as pl
from jax.experimental.pallas import tpu as pltpu
from jax.sharding import PartitionSpec as P

MESH = pl.DeviceIdType.MESH
STEPS = 2
TERMS = 8
LOOPS = 16
HORIZON = 4.0 / 3.0
EXPONENT = 16.0

NZ, NXL, NYL = 64, 8, 128
HALF = NXL // 2
REACH = TERMS - 1
OWN = REACH
WIDE = REACH + HALF
LAST = WIDE - 1
ROWS = NYL + 32
LOW, HIGH = 16, 16 + NYL
CHUNK = 8


def cheb_coeffs(term_count):
    angles = np.pi * (np.arange(term_count) + 0.5) / term_count
    cheb_nodes = np.cos(angles)
    samples = np.exp(-EXPONENT * (cheb_nodes + 1.0))
    coeffs = [
        2.0 / term_count * float(np.sum(samples * np.cos(term_index * angles)))
        for term_index in range(term_count)
    ]
    coeffs[0] = coeffs[0] / 2.0
    return coeffs


def chunks(low, high):
    return [(r, min(CHUNK, high - r)) for r in range(low, high, CHUNK)]


ALL_ROWS = (LOW - 8, HIGH + 8)
OWN_ROWS = (LOW, HIGH)


def kernel(
    sizes,
    init_hbm, cap_hbm, prof_ref, bore_ref, plan_ref, out_ref,
    nat, pool, src, xbuf, hbuf, bext, plans, rates, mom, pay, coef, sums_x, sums_y,
    load_sem, bore_send, bore_recv, plan_send, plan_recv, halo_send, halo_recv,
    sum_send, sum_recv, shift_send, shift_recv,
):
    slices, nx, ny = sizes
    slots = max(1, slices // 2)
    inv_step = STEPS * slices / HORIZON
    tm, gx, gy = lax.axis_index("tm"), lax.axis_index("gx"), lax.axis_index("gy")
    f32 = jnp.float32
    cheb = cheb_coeffs(TERMS)

    INV, DINV, U0, KU = 0, 1, 2, 3
    CA, CG = 4, 5
    X = 6
    V = X + slots
    TS = V
    ZX = V + max(3 * slots, TERMS - 1)

    def has(a, b):
        x, y = gx + a, gy + b
        return (x >= 0) & (x < nx) & (y >= 0) & (y < ny)

    around = [(a, b) for b in (-1, 0, 1) for a in (-1, 0, 1) if (a, b) != (0, 0)]
    around.sort(key=lambda ab: ab[1] == 0)
    pending = []

    load_cap = pltpu.make_async_copy(cap_hbm, nat.at[0], load_sem.at[0])
    load_init = pltpu.make_async_copy(init_hbm, nat.at[1], load_sem.at[1])
    load_cap.start()
    load_init.start()

    barrier = pltpu.get_barrier_semaphore()
    for d in range(1, nx):
        pl.semaphore_signal(barrier, inc=1, device_id={"gx": lax.rem(gx + d, nx)}, device_id_type=MESH)
    for d in range(1, ny):
        pl.semaphore_signal(barrier, inc=1, device_id={"gy": lax.rem(gy + d, ny)}, device_id_type=MESH)
    for a, b in around:
        if a and b:
            @pl.when(has(a, b))
            def _():
                pl.semaphore_signal(barrier, inc=1, device_id={"gx": gx + a, "gy": gy + b}, device_id_type=MESH)
    spans = [1] + [2 * s for s in range(1, slots)]
    for s in spans:
        @pl.when(tm >= s)
        def _():
            pl.semaphore_signal(barrier, inc=1, device_id={"tm": tm - s}, device_id_type=MESH)
    greeted = nx - 1 + ny - 1
    for a, b in around:
        if a and b:
            greeted = greeted + jnp.where(has(a, b), 1, 0)
    for s in spans:
        greeted = greeted + jnp.where(tm + s < slices, 1, 0)
    pl.semaphore_wait(barrier, greeted)

    lane = lax.broadcasted_iota(jnp.int32, (8, 128), 1)
    lane_c = lax.broadcasted_iota(jnp.int32, (CHUNK, 128), 1)

    def lanes_for(n):
        return lax.broadcasted_iota(jnp.int32, (n, 128), 1)

    plans[0] = jnp.zeros((8, 128), jnp.int32)
    plans[0, 0:STEPS, 0:LOOPS] = plan_ref[...]
    bext[1, 8:16, :] = bore_ref[...]
    for n, (a, b) in enumerate(around):
        @pl.when(has(a, b))
        def _():
            pltpu.make_async_remote_copy(
                src_ref=bore_ref, dst_ref=bext.at[1 - b, pl.ds(8 * (1 - a), 8), :],
                send_sem=bore_send.at[n], recv_sem=bore_recv.at[n],
                device_id={"gx": gx + a, "gy": gy + b}, device_id_type=MESH,
            ).start()
    for s in range(1, slots):
        @pl.when(tm + 2 * s < slices)
        def _():
            pltpu.make_async_remote_copy(
                src_ref=plans.at[0], dst_ref=plans.at[s],
                send_sem=plan_send.at[s], recv_sem=plan_recv.at[s],
                device_id={"tm": tm + 2 * s}, device_id_type=MESH,
            ).start()

    def halo_copy(e, at, n, a, b):
        rows = pl.ds(LOW, NYL) if b == 0 else pl.ds(LOW, 8) if b < 0 else pl.ds(HIGH - 8, 8)
        if a == 0:
            dst = hbuf.at[e, 1 if b < 0 else 0]
        else:
            at_rows = pl.ds(8, NYL) if b == 0 else pl.ds(8 + NYL, 8) if b < 0 else pl.ds(0, 8)
            dst = xbuf.at[e, 1 if a < 0 else 0, :, at_rows, :]
        return pltpu.make_async_remote_copy(
            src_ref=pool.at[at, pl.ds(OWN, HALF), rows, :], dst_ref=dst,
            send_sem=halo_send.at[e, n], recv_sem=halo_recv.at[e, n],
            device_id={"gx": gx + a, "gy": gy + b}, device_id_type=MESH,
        )

    def halo_start(e, at):
        for n, (a, b) in enumerate(around):
            @pl.when(has(a, b))
            def _():
                halo_copy(e, at, n, a, b).start()
        pending.append((e, at))

    def halo_wait(e, at):
        for n, (a, b) in enumerate(around):
            @pl.when(has(-a, -b))
            def _():
                halo_copy(e, at, n, a, b).wait_recv()

    left, right, down, up = gx > 0, gx < nx - 1, gy > 0, gy < ny - 1

    def edge_flag(r):
        return down if r < LOW else up if r >= HIGH else None

    def halo_build(e, at):
        def outer(m, crossed):
            for r, n in chunks(*ALL_ROWS):
                low = lanes_for(n) < NZ
                row = pl.ds(r - 8, n)
                q = (OWN - 1 - m) if crossed else m + 1
                one, two = xbuf[e, 0, q, row, :], xbuf[e, 1, q, row, :]
                from_left, from_right = (~low if crossed else low) & left, (low if crossed else ~low) & right
                if (r < LOW or r >= HIGH) and n == 8:
                    from_left, from_right = from_left & edge_flag(r), from_right & edge_flag(r)
                elif n > 8:
                    at_row = lax.broadcasted_iota(jnp.int32, (n, 128), 0) + r
                    inside = ((at_row >= LOW) | down) & ((at_row < HIGH) | up)
                    from_left, from_right = from_left & inside, from_right & inside
                value = jnp.where(from_left, one, jnp.where(from_right, two, f32(0.0)))
                if crossed:
                    value = pltpu.roll(value, NZ, 1)
                pool[at, m, pl.ds(r, n), :] = value

        def straight_row(m, _):
            outer(m, False)
            return _

        def crossed_row(m, _):
            outer(m, True)
            return _

        lax.fori_loop(0, HALF - 1, straight_row, 0)
        lax.fori_loop(HALF - 1, REACH, crossed_row, 0)
        for q in range(HALF):
            pool[at, OWN + q, LOW - 8:LOW, :] = jnp.where(down, hbuf[e, 0, q], f32(0.0))
            pool[at, OWN + q, HIGH:HIGH + 8, :] = jnp.where(up, hbuf[e, 1, q], f32(0.0))

    def to_wide(which, at):
        for q in range(HALF):
            top = nat[which, pl.ds(q, NZ, stride=NXL), :]
            low = nat[which, pl.ds(NXL - 1 - q, NZ, stride=NXL), :]
            pool[at, OWN + q, LOW:HIGH, :] = jnp.concatenate([top, low], axis=0).T

    load_cap.wait()
    to_wide(0, INV)
    halo_start(0, INV)
    load_init.wait()
    to_wide(1, U0)
    halo_start(1, U0)

    def clear(p, _):
        def row(m, __):
            pool[p, m, 0:8, :] = jnp.zeros((8, 128), f32)
            pool[p, m, ROWS - 8:ROWS, :] = jnp.zeros((8, 128), f32)
            return __
        return lax.fori_loop(0, WIDE, row, _)

    lax.fori_loop(0, ZX + 1, clear, 0)

    for sy in range(3):
        for sx in range(3):
            if (sx, sy) != (1, 1):
                @pl.when(~has(sx - 1, sy - 1))
                def _():
                    bext[sy, 8 * sx:8 * sx + 8, :] = jnp.full((8, 128), LOOPS, jnp.int32)
    for n, (a, b) in enumerate(around):
        @pl.when(has(-a, -b))
        def _():
            pltpu.make_async_remote_copy(
                src_ref=bore_ref, dst_ref=bext.at[1 - b, pl.ds(8 * (1 - a), 8), :],
                send_sem=bore_send.at[n], recv_sem=bore_recv.at[n],
                device_id={"gx": gx - a, "gy": gy - b}, device_id_type=MESH,
            ).wait_recv()
    for s in range(1, slots):
        @pl.when(tm - 2 * s >= 0)
        def _():
            pltpu.make_async_remote_copy(
                src_ref=plans.at[0], dst_ref=plans.at[s],
                send_sem=plan_send.at[s], recv_sem=plan_recv.at[s],
                device_id={"tm": tm - 2 * s}, device_id_type=MESH,
            ).wait_recv()

        @pl.when(tm - 2 * s < 0)
        def _():
            plans[s] = plans[0]

    SPAN = NYL + 16
    for s in range(slots):
        table = plans[s].astype(f32) - 3.5
        for n in range(STEPS):
            at_row = (s * STEPS + n) * SPAN
            for sy in range(3):
                loops = bext[sy]
                rate = jnp.zeros((24, 128), f32)
                for v in range(LOOPS):
                    rate = jnp.where(loops == v, jnp.broadcast_to(table[n:n + 1, v:v + 1], (24, 128)), rate)
                turned = jnp.concatenate([rate, jnp.zeros((104, 128), f32)], axis=0).T
                if sy == 0:
                    rates[at_row:at_row + 8, :] = turned[120:128, :]
                elif sy == 1:
                    rates[at_row + 8:at_row + 8 + NYL, :] = turned
                else:
                    rates[at_row + 8 + NYL:at_row + SPAN, :] = turned[0:8, :]
    depth = jnp.concatenate([prof_ref[...], prof_ref[...]], axis=1)

    def spread(m, _):
        here = m - REACH + NXL
        there = NXL - 1 - (m - REACH) + NXL
        pick_row = lax.broadcasted_iota(jnp.int32, (128, 128), 0)
        pick_lane = lax.broadcasted_iota(jnp.int32, (128, 128), 1)
        pick = jnp.where(pick_row == jnp.where(pick_lane < NZ, here, there), f32(1.0), f32(0.0))
        for q in range(slots * STEPS):
            part = rates[q * SPAN:(q + 1) * SPAN, :].astype(jnp.bfloat16)
            wide = jnp.dot(part, pick.astype(jnp.bfloat16), preferred_element_type=f32)
            src[m, q * SPAN:(q + 1) * SPAN, :] = wide * depth
        return _

    lax.fori_loop(1, WIDE, spread, 0)

    def beside(at, m, r, n, last):
        z_lane = lanes_for(n) & (NZ - 1)
        mid = pool[at, m, pl.ds(r, n), :]
        rows = pool[at, m - 1, pl.ds(r, n), :]
        rows = rows + (pltpu.roll(mid, NZ, 1) if last else pool[at, m + 1, pl.ds(r, n), :])
        cols = pool[at, m, pl.ds(r - 1, n), :] + pool[at, m, pl.ds(r + 1, n), :]
        above = jnp.where(z_lane != 0, pltpu.roll(mid, 1, 1), f32(0.0))
        below = jnp.where(z_lane != NZ - 1, pltpu.roll(mid, 127, 1), f32(0.0))
        return mid, (rows + cols) + (above + below)

    def sweep(first, body):
        def step(m, _):
            body(m, False)
            return _
        lax.fori_loop(first, LAST, step, 0)
        body(LAST, True)

    def sweep_sum(first, body, count):
        def halo(m, _):
            body(m, False, None)
            return _
        if first < OWN:
            lax.fori_loop(first, OWN, halo, 0)
        def own(m, totals):
            return body(m, False, totals)
        totals = tuple(jnp.zeros((CHUNK if CHUNK == 8 else NYL, 128), f32) for _ in range(count))
        totals = lax.fori_loop(OWN, LAST, own, totals)
        return body(LAST, True, totals)

    def is_own(r):
        return LOW <= r < HIGH

    def row_chunks(totals):
        if totals is None:
            return chunks(*ALL_ROWS)
        return [(LOW - 8, 8)] + chunks(*OWN_ROWS) + [(HIGH, 8)]

    halo_wait(0, INV)
    halo_build(0, INV)

    def invert(m, _):
        for r, n in chunks(*ALL_ROWS):
            cap = pool[INV, m, pl.ds(r, n), :]
            inside = cap > 0.0
            pool[DINV, m, pl.ds(r, n), :] = jnp.where(inside, 1.0 / (cap * f32(inv_step) + 6.0), f32(0.0))
            pool[CA, m, pl.ds(r, n), :] = jnp.where(inside, 1.0 / cap, f32(0.0))
        return _

    lax.fori_loop(0, WIDE, invert, 0)
    halo_wait(1, U0)
    halo_build(1, U0)

    def initial_image(m, last):
        for r, n in chunks(*ALL_ROWS):
            mid, total = beside(U0, m, r, n, last)
            pool[KU, m, pl.ds(r, n), :] = 6.0 * mid - total

    sweep(1, initial_image)

    def krylov(n_step, s, first):
        v = V + 3 * s
        flag = jnp.where(tm - 2 * s == 0, f32(1.0), f32(0.0))
        base = (s * STEPS + n_step) * SPAN

        def start(m, last, totals):
            for r, n in row_chunks(totals):
                source = src[m, pl.ds(pl.multiple_of(base, 8) + (r - 8), n), :]
                if n_step == 0:
                    residual = source - flag * pool[KU, m, pl.ds(r, n), :]
                else:
                    mid, total = beside(X + s, m, r, n, last)
                    residual = source - (6.0 * mid - total)
                z = pool[DINV, m, pl.ds(r, n), :] * residual
                pool[v, m, pl.ds(r, n), :] = z
                if totals is not None and is_own(r):
                    totals = (totals[0] + residual * z,)
            return totals

        def power(at, m, last, totals):
            for r, n in row_chunks(totals):
                mid, total = beside(at, m, r, n, last)
                z = pool[DINV, m, pl.ds(r, n), :] * total
                pool[at + 1, m, pl.ds(r, n), :] = z
                if totals is not None and is_own(r):
                    totals = (totals[0] + mid * total, totals[1] + z * total)
            return totals

        def final(m, last, totals):
            for r, n in chunks(*OWN_ROWS):
                mid, total = beside(v + 2, m, r, n, last)
                totals = (totals[0] + mid * total,)
            return totals

        sums = list(sweep_sum(first, start, 1))
        sums += sweep_sum(first + 1, functools.partial(power, v), 2)
        sums += sweep_sum(first + 2, functools.partial(power, v + 1), 2)
        sums += sweep_sum(OWN, final, 1)
        for j, total in enumerate(sums):
            mom[n_step, j, pl.ds(s, 1), :] = jnp.sum(total, axis=0, keepdims=True)

    def total_over_tiles(n_step):
        packed = jnp.zeros((8, 128), f32)
        for j in range(6):
            packed = jnp.where(lane == j, jnp.sum(mom[n_step, j], axis=1, keepdims=True), packed)
        for stage, (axis, count, me, buf) in enumerate((("gx", nx, gx, sums_x), ("gy", ny, gy, sums_y))):
            pay[n_step, stage] = packed
            copies = []
            for d in range(1, count):
                copies.append(pltpu.make_async_remote_copy(
                    src_ref=pay.at[n_step, stage], dst_ref=buf.at[n_step, d],
                    send_sem=sum_send.at[n_step, stage, d], recv_sem=sum_recv.at[n_step, stage, d],
                    device_id={axis: lax.rem(me + d, count)}, device_id_type=MESH,
                ))
                copies[-1].start()
            for d, copy in enumerate(copies):
                copy.wait_recv()
                packed = packed + buf[n_step, d + 1]
            for copy in copies:
                copy.wait_send()
        return [jnp.broadcast_to(packed[:, j:j + 1], (8, 128)) for j in range(6)]

    def cg_coefficients(mu):
        def inner(p, q, m):
            total = None
            for i, a in enumerate(p):
                for j, b in enumerate(q):
                    term = a * b * m[i + j]
                    total = term if total is None else total + term
            return total

        gap = [mu[j] - mu[j + 1] for j in range(5)]
        one = jnp.ones((8, 128), f32)
        x = [jnp.zeros((8, 128), f32)] * 3
        z, direction = [one], [one]
        inner_now = mu[0]
        for it in range(3):
            step = inner_now / inner(direction, direction, gap)
            x = [x[i] + step * direction[i] if i < len(direction) else x[i] for i in range(3)]
            if it < 2:
                grown = direction + [jnp.zeros((8, 128), f32)]
                shifted = [jnp.zeros((8, 128), f32)] + direction
                z = [(z[i] if i < len(z) else 0.0) - step * (grown[i] - shifted[i]) for i in range(len(grown))]
                inner_next = inner(z, z, mu)
                ratio = inner_next / inner_now
                direction = [z[i] + ratio * direction[i] if i < len(direction) else z[i] for i in range(len(z))]
                inner_now = inner_next
        return x

    for n_step, first in ((0, 1), (1, 4)):
        def each(s, _):
            krylov(n_step, s, first)
            return _

        mom[n_step] = jnp.zeros((6, 8, 128), f32)
        lax.fori_loop(0, slots, each, 0)
        weights = cg_coefficients(total_over_tiles(n_step))
        for i in range(3):
            coef[n_step, i] = weights[i]

        def update(s, _):
            w = [coef[n_step, i, pl.ds(s, 1), :] for i in range(3)]
            flag = jnp.where(tm - 2 * s == 0, f32(1.0), f32(0.0))

            def row(m, _):
                for r, n in chunks(*(ALL_ROWS if n_step == 0 else OWN_ROWS)):
                    value = w[0] * pool[V + 3 * s, m, pl.ds(r, n), :]
                    value = value + w[1] * pool[V + 3 * s + 1, m, pl.ds(r, n), :]
                    value = value + w[2] * pool[V + 3 * s + 2, m, pl.ds(r, n), :]
                    if n_step == 0:
                        value = value + flag * pool[U0, m, pl.ds(r, n), :]
                    else:
                        value = jnp.where(tm - 2 * s >= 0, value + pool[X + s, m, pl.ds(r, n), :], f32(0.0))
                    pool[X + s, m, pl.ds(r, n), :] = value
                return _

            return lax.fori_loop(3 if n_step == 0 else OWN, WIDE, row, _)

        lax.fori_loop(0, slots, update, 0)

    def shift_factors(scale):
        def row(m, _):
            for r, n in chunks(*ALL_ROWS):
                a = pool[KU, m, pl.ds(r, n), :] * f32(2.0 * scale)
                pool[CA, m, pl.ds(r, n), :] = a
                pool[CG, m, pl.ds(r, n), :] = 6.0 * a - 2.0
            return _
        lax.fori_loop(0, WIDE, row, 0)

    def keep(m, _):
        for r, n in chunks(*ALL_ROWS):
            pool[KU, m, pl.ds(r, n), :] = pool[CA, m, pl.ds(r, n), :]
        return _

    lax.fori_loop(0, WIDE, keep, 0)

    def propagate(at, to):
        def first_term(m, last):
            for r, n in chunks(*ALL_ROWS):
                mid, total = beside(at, m, r, n, last)
                pool[TS, m, pl.ds(r, n), :] = 0.5 * (pool[CG, m, pl.ds(r, n), :] * mid - pool[CA, m, pl.ds(r, n), :] * total)

        def term(before, now, m, last, rows):
            out = []
            for r, n in chunks(*rows):
                mid, total = beside(now, m, r, n, last)
                out.append((r, n, mid, pool[CG, m, pl.ds(r, n), :] * mid - pool[CA, m, pl.ds(r, n), :] * total
                            - pool[before, m, pl.ds(r, n), :]))
            return out

        def store(before, now, into, m, last):
            for r, n in chunks(*ALL_ROWS):
                mid, total = beside(now, m, r, n, last)
                pool[into, m, pl.ds(r, n), :] = (
                    pool[CG, m, pl.ds(r, n), :] * mid - pool[CA, m, pl.ds(r, n), :] * total
                    - pool[before, m, pl.ds(r, n), :])

        def add_up(m, last):
            for r, n in chunks(*OWN_ROWS):
                mid, total = beside(TS + 5, m, r, n, last)
                final = pool[CG, m, pl.ds(r, n), :] * mid - pool[CA, m, pl.ds(r, n), :] * total - pool[TS + 4, m, pl.ds(r, n), :]
                value = f32(cheb[0]) * pool[at, m, pl.ds(r, n), :] + f32(cheb[7]) * final + f32(cheb[6]) * mid
                for j in range(1, 6):
                    value = value + f32(cheb[j]) * pool[TS + j - 1, m, pl.ds(r, n), :]
                pool[to, m, pl.ds(r, n), :] = pool[to, m, pl.ds(r, n), :] + value

        sweep(1, first_term)
        sweep(2, functools.partial(store, at, TS, TS + 1))

        def later(j, _):
            sweep(j, functools.partial(store, TS + j - 3, TS + j - 2, TS + j - 1))
            return _

        lax.fori_loop(3, 7, later, 0)
        sweep(OWN, add_up)

    scale_one = 1.0 / (12.0 * slices)
    e = 2
    started = {}

    def start_slot(s):
        nonlocal e
        halo_start(e, X + s)
        started[s] = e
        e += 1

    span = slots // 2
    ready = {}
    while span >= 1:
        todo = [s for s in range(slots - 1, -1, -1) if s >= span and s < 2 * span]
        for s in todo:
            if s not in started:
                start_slot(s)
        shift_factors(2 * span * scale_one)
        for s in todo:
            halo_wait(started[s], X + s)
            halo_build(started[s], X + s)
            propagate(X + s, X + s - span)
            if s - span >= span // 2 and s - span < span and span > 1 and s - span > 0:
                start_slot(s - span)
        span //= 2

    shift = pltpu.make_async_remote_copy(
        src_ref=pool.at[X, pl.ds(OWN, HALF), pl.ds(LOW, NYL), :],
        dst_ref=pool.at[ZX, pl.ds(OWN, HALF), pl.ds(LOW, NYL), :],
        send_sem=shift_send.at[0], recv_sem=shift_recv.at[0],
        device_id={"tm": lax.rem(tm + 1, slices)}, device_id_type=MESH,
    )

    @pl.when(tm < slices - 1)
    def _():
        shift.start()

    shift_factors(scale_one)

    @pl.when(tm > 0)
    def _():
        shift.wait_recv()

    @pl.when(tm == 0)
    def _():
        pool[ZX, OWN:WIDE, LOW:HIGH, :] = jnp.zeros((HALF, NYL, 128), f32)

    halo_start(e, ZX)
    halo_wait(e, ZX)
    halo_build(e, ZX)

    @pl.when(tm < slices - 1)
    def _():
        shift.wait_send()

    propagate(ZX, X)

    for q in range(HALF):
        turned = pool[X, OWN + q, LOW:HIGH, :].T
        nat[1, pl.ds(q, NZ, stride=NXL), :] = turned[0:NZ, :]
        nat[1, pl.ds(NXL - 1 - q, NZ, stride=NXL), :] = turned[NZ:2 * NZ, :]
    store_out = pltpu.make_async_copy(nat.at[1], out_ref, load_sem.at[2])
    store_out.start()

    for n, (a, b) in enumerate(around):
        @pl.when(has(a, b))
        def _():
            pltpu.make_async_remote_copy(
                src_ref=bore_ref, dst_ref=bext.at[1 - b, pl.ds(8 * (1 - a), 8), :],
                send_sem=bore_send.at[n], recv_sem=bore_recv.at[n],
                device_id={"gx": gx + a, "gy": gy + b}, device_id_type=MESH,
            ).wait_send()
            for e_done, at in pending:
                halo_copy(e_done, at, n, a, b).wait_send()
    for s in range(1, slots):
        @pl.when(tm + 2 * s < slices)
        def _():
            pltpu.make_async_remote_copy(
                src_ref=plans.at[0], dst_ref=plans.at[s],
                send_sem=plan_send.at[s], recv_sem=plan_recv.at[s],
                device_id={"tm": tm + 2 * s}, device_id_type=MESH,
            ).wait_send()
    store_out.wait()


def per_device(sizes, initial, capacity, profile, bore_loop, plan):
    slices = sizes[0]
    slots = max(1, slices // 2)
    exchanges = 2 + (slots - 1) + 1
    pool_size = 6 + slots + max(3 * slots, TERMS - 1) + 1
    f32 = jnp.float32
    dma = pltpu.SemaphoreType.DMA
    out = pl.pallas_call(
        functools.partial(kernel, sizes),
        out_shape=jax.ShapeDtypeStruct((NZ * NXL, NYL), f32),
        in_specs=[
            pl.BlockSpec(memory_space=pl.ANY),
            pl.BlockSpec(memory_space=pl.ANY),
            pl.BlockSpec(memory_space=pltpu.VMEM),
            pl.BlockSpec(memory_space=pltpu.VMEM),
            pl.BlockSpec(memory_space=pltpu.VMEM),
        ],
        out_specs=pl.BlockSpec(memory_space=pl.ANY),
        scratch_shapes=[
            pltpu.VMEM((2, NZ * NXL, NYL), f32),
            pltpu.VMEM((pool_size, WIDE, ROWS, 128), f32),
            pltpu.VMEM((WIDE, slots * STEPS * (NYL + 16), 128), f32),
            pltpu.VMEM((exchanges, 2, HALF, NYL + 16, 128), f32),
            pltpu.VMEM((exchanges, 2, HALF, 8, 128), f32),
            pltpu.VMEM((3, 24, 128), jnp.int32),
            pltpu.VMEM((slots, 8, 128), jnp.int32),
            pltpu.VMEM((slots * STEPS * (NYL + 16), 128), f32),
            pltpu.VMEM((STEPS, 6, 8, 128), f32),
            pltpu.VMEM((STEPS, 2, 8, 128), f32),
            pltpu.VMEM((STEPS, 3, 8, 128), f32),
            pltpu.VMEM((STEPS, 8, 8, 128), f32),
            pltpu.VMEM((STEPS, 8, 8, 128), f32),
            dma((3,)),
            dma((8,)),
            dma((8,)),
            dma((slots,)),
            dma((slots,)),
            dma((exchanges, 8)),
            dma((exchanges, 8)),
            dma((STEPS, 2, 8)),
            dma((STEPS, 2, 8)),
            dma((1,)),
            dma((1,)),
        ],
        compiler_params=pltpu.CompilerParams(
            collective_id=0, has_side_effects=True, vmem_limit_bytes=56 * 1024 * 1024
        ),
    )(
        initial.reshape(NZ * NXL, NYL),
        capacity.reshape(NZ * NXL, NYL),
        profile.reshape(1, NZ),
        bore_loop,
        plan[0],
    )
    return out.reshape(1, NZ, NXL, NYL)


def solution(mesh):
    sizes = (mesh.shape["tm"], mesh.shape["gx"], mesh.shape["gy"])
    return jax.shard_map(
        functools.partial(per_device, sizes),
        mesh=mesh,
        in_specs=(
            P(None, "gx", "gy"),
            P(None, "gx", "gy"),
            P(),
            P("gx", "gy"),
            P("tm", None, None),
        ),
        out_specs=P("tm", None, "gx", "gy"),
        check_vma=False,
    )
```

```python
import functools

import jax
import jax.numpy as jnp
import numpy as np
from jax import lax
from jax.experimental import pallas as pl
from jax.experimental.pallas import tpu as pltpu
from jax.sharding import PartitionSpec as P

MESH = pl.DeviceIdType.MESH
STEPS = 2
TERMS = 8
LOOPS = 16
HORIZON = 4.0 / 3.0
EXPONENT = 16.0

NZ, NXL, NYL = 64, 8, 128
HALF = NXL // 2
REACH = TERMS - 1
OWN = REACH
WIDE = REACH + HALF
LAST = WIDE - 1
ROWS = NYL + 32
LOW, HIGH = 16, 16 + NYL
CHUNK = 16


def cheb_coeffs(term_count):
    angles = np.pi * (np.arange(term_count) + 0.5) / term_count
    cheb_nodes = np.cos(angles)
    samples = np.exp(-EXPONENT * (cheb_nodes + 1.0))
    coeffs = [
        2.0 / term_count * float(np.sum(samples * np.cos(term_index * angles)))
        for term_index in range(term_count)
    ]
    coeffs[0] = coeffs[0] / 2.0
    return coeffs


def chunks(low, high, size):
    return [(r, min(size, high - r)) for r in range(low, high, size)]


def kernel(
    sizes,
    init_hbm, cap_hbm, prof_ref, bore_ref, plan_ref, out_ref,
    nat, src, xbuf, hbuf, bext, plans, rates, mom, pay, coef, sums_x, sums_y,
    load_sem, bore_send, bore_recv, plan_send, plan_recv, halo_send, halo_recv,
    sum_send, sum_recv, shift_send, shift_recv,
    heat, inv, dinv, u0, ku, ca, cg, xs, v0s, v1s, v2s, *ts,
):
    slices, nx, ny = sizes
    slots = max(1, slices // 2)
    inv_step = STEPS * slices / HORIZON
    tm, gx, gy = lax.axis_index("tm"), lax.axis_index("gx"), lax.axis_index("gy")
    f32 = jnp.float32
    cheb = cheb_coeffs(TERMS)

    def has(a, b):
        x, y = gx + a, gy + b
        return (x >= 0) & (x < nx) & (y >= 0) & (y < ny)

    around = [(a, b) for b in (-1, 0, 1) for a in (-1, 0, 1) if (a, b) != (0, 0)]
    around.sort(key=lambda ab: ab[1] == 0)

    load_cap = pltpu.make_async_copy(cap_hbm, nat.at[0], load_sem.at[0])
    load_init = pltpu.make_async_copy(init_hbm, nat.at[1], load_sem.at[1])
    load_cap.start()
    load_init.start()

    barrier = pltpu.get_barrier_semaphore()
    for d in range(1, nx):
        pl.semaphore_signal(barrier, inc=1, device_id={"gx": lax.rem(gx + d, nx)}, device_id_type=MESH)
    for d in range(1, ny):
        pl.semaphore_signal(barrier, inc=1, device_id={"gy": lax.rem(gy + d, ny)}, device_id_type=MESH)
    for a, b in around:
        if a and b:
            @pl.when(has(a, b))
            def _():
                pl.semaphore_signal(barrier, inc=1, device_id={"gx": gx + a, "gy": gy + b}, device_id_type=MESH)
    spans = [1] + [2 * s for s in range(1, slots)]
    for s in spans:
        @pl.when(tm >= s)
        def _():
            pl.semaphore_signal(barrier, inc=1, device_id={"tm": tm - s}, device_id_type=MESH)
    greeted = nx - 1 + ny - 1
    for a, b in around:
        if a and b:
            greeted = greeted + jnp.where(has(a, b), 1, 0)
    for s in spans:
        greeted = greeted + jnp.where(tm + s < slices, 1, 0)
    pl.semaphore_wait(barrier, greeted)

    lane = lax.broadcasted_iota(jnp.int32, (8, 128), 1)

    plans[0] = jnp.zeros((8, 128), jnp.int32)
    plans[0, 0:STEPS, 0:LOOPS] = plan_ref[...]
    bext[1, 8:16, :] = bore_ref[...]
    for n, (a, b) in enumerate(around):
        @pl.when(has(a, b))
        def _():
            pltpu.make_async_remote_copy(
                src_ref=bore_ref, dst_ref=bext.at[1 - b, pl.ds(8 * (1 - a), 8), :],
                send_sem=bore_send.at[n], recv_sem=bore_recv.at[n],
                device_id={"gx": gx + a, "gy": gy + b}, device_id_type=MESH,
            ).start()
    for s in range(1, slots):
        @pl.when(tm + 2 * s < slices)
        def _():
            pltpu.make_async_remote_copy(
                src_ref=plans.at[0], dst_ref=plans.at[s],
                send_sem=plan_send.at[s], recv_sem=plan_recv.at[s],
                device_id={"tm": tm + 2 * s}, device_id_type=MESH,
            ).start()

    def halo_copy(e, at, n, a, b):
        rows = pl.ds(LOW, NYL) if b == 0 else pl.ds(LOW, 8) if b < 0 else pl.ds(HIGH - 8, 8)
        if a == 0:
            dst = hbuf.at[e, 1 if b < 0 else 0]
        else:
            at_rows = pl.ds(8, NYL) if b == 0 else pl.ds(8 + NYL, 8) if b < 0 else pl.ds(0, 8)
            dst = xbuf.at[e, 1 if a < 0 else 0, :, at_rows, :]
        return pltpu.make_async_remote_copy(
            src_ref=at.at[pl.ds(OWN, HALF), rows, :], dst_ref=dst,
            send_sem=halo_send.at[e, n], recv_sem=halo_recv.at[e, n],
            device_id={"gx": gx + a, "gy": gy + b}, device_id_type=MESH,
        )

    def halo_start(e, at):
        for n, (a, b) in enumerate(around):
            @pl.when(has(a, b))
            def _():
                halo_copy(e, at, n, a, b).start()

    def halo_wait(e, at):
        for n, (a, b) in enumerate(around):
            @pl.when(has(-a, -b))
            def _():
                halo_copy(e, at, n, a, b).wait_recv()

    left, right, down, up = gx > 0, gx < nx - 1, gy > 0, gy < ny - 1

    low_lanes = lax.broadcasted_iota(jnp.int32, (1, 8, 128), 2) < NZ

    def halo_build(e, at):
        for r, n in [(0, 8), (8, NYL), (8 + NYL, 8)]:
            edge = down if r == 0 else up if r > 8 else True
            for crossed in (False, True):
                from_left = (~low_lanes if crossed else low_lanes) & left & edge
                from_right = (low_lanes if crossed else ~low_lanes) & right & edge
                for m in range(HALF - 1, REACH) if crossed else range(HALF - 1):
                    q = REACH - 1 - m if crossed else m + 1
                    one = xbuf[e, 0, q, r:r + n, :].reshape(n // 8, 8, 128)
                    two = xbuf[e, 1, q, r:r + n, :].reshape(n // 8, 8, 128)
                    value = jnp.where(from_left, one, jnp.where(from_right, two, f32(0.0)))
                    if crossed:
                        value = pltpu.roll(value, NZ, 2)
                    at[m, LOW - 8 + r:LOW - 8 + r + n, :] = value.reshape(n, 128)
        at[OWN:WIDE, LOW - 8:LOW, :] = jnp.where(down, hbuf[e, 0], f32(0.0))
        at[OWN:WIDE, HIGH:HIGH + 8, :] = jnp.where(up, hbuf[e, 1], f32(0.0))

    def to_wide(which, at):
        for q in range(HALF):
            top = nat[which, pl.ds(q, NZ, stride=NXL), :]
            low = nat[which, pl.ds(NXL - 1 - q, NZ, stride=NXL), :]
            at[OWN + q, LOW:HIGH, :] = jnp.concatenate([top, low], axis=0).T

    load_cap.wait()
    to_wide(0, heat)
    halo_start(0, heat)
    load_init.wait()
    to_wide(1, u0)
    halo_start(1, u0)

    for sy in range(3):
        for sx in range(3):
            if (sx, sy) != (1, 1):
                @pl.when(~has(sx - 1, sy - 1))
                def _():
                    bext[sy, 8 * sx:8 * sx + 8, :] = jnp.full((8, 128), LOOPS, jnp.int32)
    for n, (a, b) in enumerate(around):
        @pl.when(has(-a, -b))
        def _():
            pltpu.make_async_remote_copy(
                src_ref=bore_ref, dst_ref=bext.at[1 - b, pl.ds(8 * (1 - a), 8), :],
                send_sem=bore_send.at[n], recv_sem=bore_recv.at[n],
                device_id={"gx": gx - a, "gy": gy - b}, device_id_type=MESH,
            ).wait_recv()
    for s in range(1, slots):
        @pl.when(tm - 2 * s >= 0)
        def _():
            pltpu.make_async_remote_copy(
                src_ref=plans.at[0], dst_ref=plans.at[s],
                send_sem=plan_send.at[s], recv_sem=plan_recv.at[s],
                device_id={"tm": tm - 2 * s}, device_id_type=MESH,
            ).wait_recv()

        @pl.when(tm - 2 * s < 0)
        def _():
            plans[s] = plans[0]

    SPAN = NYL + 16
    loops = jnp.concatenate([bext[0], bext[1], bext[2]], axis=0)
    for s in range(slots):
        table = plans[s].astype(f32) - 3.5
        for n in range(STEPS):
            at_row = (s * STEPS + n) * SPAN
            rate = jnp.zeros((72, 128), f32)
            for v in range(LOOPS):
                rate = jnp.where(loops == v, jnp.broadcast_to(table[n:n + 1, v:v + 1], (72, 128)), rate)
            turned = jnp.concatenate([rate, jnp.zeros((56, 128), f32)], axis=0).T
            rates[at_row:at_row + 8, :] = pltpu.roll(turned[120:128, :], 24, 1)
            rates[at_row + 8:at_row + 8 + NYL, :] = turned
            rates[at_row + 8 + NYL:at_row + SPAN, :] = pltpu.roll(turned[0:8, :], 104, 1)
    depth = jnp.concatenate([prof_ref[...], prof_ref[...]], axis=1)

    def spread(m, _):
        here = 32 + m - REACH
        there = 32 + NXL - 1 - (m - REACH)
        pick_row = lax.broadcasted_iota(jnp.int32, (128, 128), 0)
        pick_lane = lax.broadcasted_iota(jnp.int32, (128, 128), 1)
        pick = jnp.where(pick_row == jnp.where(pick_lane < NZ, here, there), f32(1.0), f32(0.0)).astype(jnp.bfloat16)
        wide = jnp.dot(rates[...].astype(jnp.bfloat16), pick, preferred_element_type=f32)
        src[m] = wide * depth
        return _

    lax.fori_loop(1, WIDE, spread, 0)

    def rolled(value, by):
        return pltpu.roll(value, by, 2)

    def beside(at, first, r, n):
        count = WIDE - first
        mid = at[first:WIDE, r:r + n, :]
        before = jnp.concatenate([at[first - 1:first, r:r + n, :], mid[:-1]], axis=0) if count > 1 else at[first - 1:first, r:r + n, :]
        across = rolled(mid[-1:], NZ)
        after = jnp.concatenate([mid[1:], across], axis=0) if count > 1 else across
        cols = at[first:WIDE, r - 1:r - 1 + n, :] + at[first:WIDE, r + 1:r + 1 + n, :]
        z_lane = lax.broadcasted_iota(jnp.int32, (count, n, 128), 2) & (NZ - 1)
        above = jnp.where(z_lane != 0, rolled(mid, 1), f32(0.0))
        below = jnp.where(z_lane != NZ - 1, rolled(mid, 127), f32(0.0))
        return mid, ((before + after) + cols) + (above + below)

    def blocks(first, wide):
        return chunks(LOW - 8, HIGH + 8, CHUNK) if wide else chunks(LOW, HIGH, CHUNK)

    def add_own(total, value, first, r, n):
        value = value[OWN - first:]
        low, high = max(LOW - r, 0), min(HIGH - r, n)
        if high <= low:
            return total
        value = value[:, low:high, :]
        return total + jnp.sum(value.reshape(-1, 8, 128), axis=0)

    halo_wait(0, heat)
    halo_build(0, heat)

    for r, n in chunks(LOW - 8, HIGH + 8, CHUNK):
        cap = heat[:, r:r + n, :]
        inside = cap > 0.0
        dinv[:, r:r + n, :] = jnp.where(inside, 1.0 / (cap * f32(inv_step) + 6.0), f32(0.0))
        inv[:, r:r + n, :] = jnp.where(inside, 1.0 / cap, f32(0.0))

    halo_wait(1, u0)
    halo_build(1, u0)
    for r, n in blocks(1, True):
        mid, total = beside(u0, 1, r, n)
        ku[1:WIDE, r:r + n, :] = 6.0 * mid - total

    zero = jnp.zeros((8, 128), f32)

    def krylov(n_step, s, first):
        x, v0, v1, v2 = xs.at[s], v0s.at[s], v1s.at[s], v2s.at[s]
        flag = jnp.where(tm - 2 * s == 0, f32(1.0), f32(0.0))
        base = s * (STEPS * SPAN) + n_step * SPAN
        sums = [zero] * 6
        for r, n in blocks(first, True):
            residual = src[first:WIDE, pl.ds(pl.multiple_of(base + (r - 8), 8), n), :]
            if n_step == 0:
                residual = residual - flag * ku[first:WIDE, r:r + n, :]
            else:
                mid, total = beside(x, first, r, n)
                residual = residual - (6.0 * mid - total)
            z = dinv[first:WIDE, r:r + n, :] * residual
            v0[first:WIDE, r:r + n, :] = z
            sums[0] = add_own(sums[0], residual * z, first, r, n)
        for k, (now, then) in enumerate(((v0, v1), (v1, v2))):
            begin = first + 1 + k
            for r, n in blocks(begin, True):
                mid, total = beside(now, begin, r, n)
                z = dinv[begin:WIDE, r:r + n, :] * total
                then[begin:WIDE, r:r + n, :] = z
                sums[2 * k + 1] = add_own(sums[2 * k + 1], mid * total, begin, r, n)
                sums[2 * k + 2] = add_own(sums[2 * k + 2], z * total, begin, r, n)
        for r, n in blocks(OWN, False):
            mid, total = beside(v2, OWN, r, n)
            sums[5] = add_own(sums[5], mid * total, OWN, r, n)
        for j, total in enumerate(sums):
            mom[n_step, j, pl.ds(s, 1), :] = jnp.sum(total, axis=0, keepdims=True)

    def total_over_tiles(n_step):
        packed = jnp.zeros((8, 128), f32)
        for j in range(6):
            packed = jnp.where(lane == j, jnp.sum(mom[n_step, j], axis=1, keepdims=True), packed)
        for stage, (axis, count, me, buf) in enumerate((("gx", nx, gx, sums_x), ("gy", ny, gy, sums_y))):
            pay[n_step, stage] = packed
            copies = []
            for d in range(1, count):
                copies.append(pltpu.make_async_remote_copy(
                    src_ref=pay.at[n_step, stage], dst_ref=buf.at[n_step, d],
                    send_sem=sum_send.at[n_step, stage, d], recv_sem=sum_recv.at[n_step, stage, d],
                    device_id={axis: lax.rem(me + d, count)}, device_id_type=MESH,
                ))
                copies[-1].start()
            for d, copy in enumerate(copies):
                copy.wait_recv()
                packed = packed + buf[n_step, d + 1]
            for copy in copies:
                copy.wait_send()
        return [jnp.broadcast_to(packed[:, j:j + 1], (8, 128)) for j in range(6)]

    def cg_coefficients(mu):
        def inner(p, q, m):
            total = None
            for i, a in enumerate(p):
                for j, b in enumerate(q):
                    term = a * b * m[i + j]
                    total = term if total is None else total + term
            return total

        gap = [mu[j] - mu[j + 1] for j in range(5)]
        one = jnp.ones((8, 128), f32)
        x = [jnp.zeros((8, 128), f32)] * 3
        z, direction = [one], [one]
        inner_now = mu[0]
        for it in range(3):
            step = inner_now / inner(direction, direction, gap)
            x = [x[i] + step * direction[i] if i < len(direction) else x[i] for i in range(3)]
            if it < 2:
                grown = direction + [jnp.zeros((8, 128), f32)]
                shifted = [jnp.zeros((8, 128), f32)] + direction
                z = [(z[i] if i < len(z) else 0.0) - step * (grown[i] - shifted[i]) for i in range(len(grown))]
                inner_next = inner(z, z, mu)
                ratio = inner_next / inner_now
                direction = [z[i] + ratio * direction[i] if i < len(direction) else z[i] for i in range(len(z))]
                inner_now = inner_next
        return x

    for n_step, first in ((0, 1), (1, 4)):
        def each(s, _):
            krylov(n_step, s, first)
            return _

        mom[n_step] = jnp.zeros((6, 8, 128), f32)
        lax.fori_loop(0, slots, each, 0)
        weights = cg_coefficients(total_over_tiles(n_step))
        for i in range(3):
            coef[n_step, i] = weights[i]

        def update(s, _):
            w = [coef[n_step, i, pl.ds(s, 1), :].reshape(1, 1, 128) for i in range(3)]
            flag = jnp.where(tm - 2 * s == 0, f32(1.0), f32(0.0))
            begin = 3 if n_step == 0 else OWN
            for r, n in blocks(begin, n_step == 0):
                here = (s, slice(begin, WIDE), slice(r, r + n))
                value = w[0] * v0s[here] + w[1] * v1s[here] + w[2] * v2s[here]
                if n_step == 0:
                    xs[here] = value + flag * u0[begin:WIDE, r:r + n, :]
                else:
                    xs[here] = jnp.where(tm - 2 * s >= 0, value + xs[here], f32(0.0))
            return _

        lax.fori_loop(0, slots, update, 0)

    plan_rows = []
    span = slots // 2
    while span >= 1:
        for s in range(2 * span - 1, span - 1, -1):
            plan_rows.append((s, s - span, 2 * span))
        span //= 2
    plan_rows.append((slots, 0, 1))
    order = [row[0] for row in plan_rows]
    last = len(plan_rows) - 1
    finished = {s: max((p for p, row in enumerate(plan_rows) if row[1] == s), default=-1) for s in order[:-1]}

    def pick(p, values):
        out = values[-1]
        for i in range(len(values) - 2, -1, -1):
            out = jnp.where(p == i, values[i], out)
        return out

    shift = pltpu.make_async_remote_copy(
        src_ref=xs.at[0, pl.ds(OWN, HALF), pl.ds(LOW, NYL), :],
        dst_ref=xs.at[slots, pl.ds(OWN, HALF), pl.ds(LOW, NYL), :],
        send_sem=shift_send.at[0], recv_sem=shift_recv.at[0],
        device_id={"tm": lax.rem(tm + 1, slices)}, device_id_type=MESH,
    )

    def pass_on():
        @pl.when(tm < slices - 1)
        def _():
            shift.start()

        @pl.when(tm == 0)
        def _():
            xs[slots, OWN:WIDE, LOW:HIGH, :] = jnp.zeros((HALF, NYL, 128), f32)

        @pl.when(tm > 0)
        def _():
            shift.wait_recv()

        halo_start(2 + last, xs.at[slots])

        @pl.when(tm < slices - 1)
        def _():
            shift.wait_send()

    for s in order[:-1]:
        if finished[s] < 0:
            halo_start(2 + order.index(s), xs.at[s])
    if last == 0:
        pass_on()

    def combine(before, now, first, r, n):
        mid, total = beside(now, first, r, n)
        return mid, cg[first:WIDE, r:r + n, :] * mid - ca[first:WIDE, r:r + n, :] * total, before[first:WIDE, r:r + n, :] if before is not None else None

    def section(p, carry):
        at, to = pick(p, order), pick(p, [row[1] for row in plan_rows])
        factor = pick(p, [jnp.float32(2.0 * row[2] / (12.0 * slices)) for row in plan_rows])
        for r, n in chunks(LOW - 8, HIGH + 8, CHUNK):
            a = inv[:, r:r + n, :] * factor
            ca[:, r:r + n, :] = a
            cg[:, r:r + n, :] = 6.0 * a - 2.0
        ts[0][OWN:WIDE, LOW:HIGH, :] = xs[at, OWN:WIDE, LOW:HIGH, :]
        halo_wait(2 + p, xs.at[at])
        halo_build(2 + p, ts[0])
        for j in range(1, TERMS - 1):
            for r, n in blocks(j, True):
                mid, value, before = combine(ts[j - 2] if j > 1 else None, ts[j - 1], j, r, n)
                ts[j][j:WIDE, r:r + n, :] = 0.5 * value if j == 1 else value - before
        for r, n in blocks(OWN, False):
            mid, value, before = combine(ts[5], ts[6], OWN, r, n)
            value = f32(cheb[7]) * (value - before) + f32(cheb[6]) * mid + f32(cheb[5]) * before
            for j in range(5):
                value = value + f32(cheb[j]) * ts[j][OWN:WIDE, r:r + n, :]
            xs[to, OWN:WIDE, r:r + n, :] = xs[to, OWN:WIDE, r:r + n, :] + value
        for s, p_done in finished.items():
            if p_done >= 0:
                @pl.when(p == p_done)
                def _():
                    halo_start(2 + order.index(s), xs.at[s])
        if last > 0:
            @pl.when(p == last - 1)
            def _():
                pass_on()
        return carry

    lax.fori_loop(0, last + 1, section, 0)

    for q in range(HALF):
        turned = xs[0, OWN + q, LOW:HIGH, :].T
        nat[1, pl.ds(q, NZ, stride=NXL), :] = turned[0:NZ, :]
        nat[1, pl.ds(NXL - 1 - q, NZ, stride=NXL), :] = turned[NZ:2 * NZ, :]
    store_out = pltpu.make_async_copy(nat.at[1], out_ref, load_sem.at[2])
    store_out.start()

    for n, (a, b) in enumerate(around):
        @pl.when(has(a, b))
        def _():
            pltpu.make_async_remote_copy(
                src_ref=bore_ref, dst_ref=bext.at[1 - b, pl.ds(8 * (1 - a), 8), :],
                send_sem=bore_send.at[n], recv_sem=bore_recv.at[n],
                device_id={"gx": gx + a, "gy": gy + b}, device_id_type=MESH,
            ).wait_send()
            halo_copy(0, heat, n, a, b).wait_send()
            halo_copy(1, u0, n, a, b).wait_send()
            for p, s in enumerate(order):
                halo_copy(2 + p, xs.at[s], n, a, b).wait_send()
    for s in range(1, slots):
        @pl.when(tm + 2 * s < slices)
        def _():
            pltpu.make_async_remote_copy(
                src_ref=plans.at[0], dst_ref=plans.at[s],
                send_sem=plan_send.at[s], recv_sem=plan_recv.at[s],
                device_id={"tm": tm + 2 * s}, device_id_type=MESH,
            ).wait_send()
    store_out.wait()


def per_device(sizes, initial, capacity, profile, bore_loop, plan):
    slices = sizes[0]
    slots = max(1, slices // 2)
    exchanges = 2 + (slots - 1) + 1
    wide = (WIDE, ROWS, 128)
    f32 = jnp.float32
    dma = pltpu.SemaphoreType.DMA
    out = pl.pallas_call(
        functools.partial(kernel, sizes),
        out_shape=jax.ShapeDtypeStruct((NZ * NXL, NYL), f32),
        in_specs=[
            pl.BlockSpec(memory_space=pl.ANY),
            pl.BlockSpec(memory_space=pl.ANY),
            pl.BlockSpec(memory_space=pltpu.VMEM),
            pl.BlockSpec(memory_space=pltpu.VMEM),
            pl.BlockSpec(memory_space=pltpu.VMEM),
        ],
        out_specs=pl.BlockSpec(memory_space=pl.ANY),
        scratch_shapes=[
            pltpu.VMEM((2, NZ * NXL, NYL), f32),
            pltpu.VMEM((WIDE, slots * STEPS * (NYL + 16), 128), f32),
            pltpu.VMEM((exchanges, 2, HALF, NYL + 16, 128), f32),
            pltpu.VMEM((exchanges, 2, HALF, 8, 128), f32),
            pltpu.VMEM((3, 24, 128), jnp.int32),
            pltpu.VMEM((slots, 8, 128), jnp.int32),
            pltpu.VMEM((slots * STEPS * (NYL + 16), 128), f32),
            pltpu.VMEM((STEPS, 6, 8, 128), f32),
            pltpu.VMEM((STEPS, 2, 8, 128), f32),
            pltpu.VMEM((STEPS, 3, 8, 128), f32),
            pltpu.VMEM((STEPS, 8, 8, 128), f32),
            pltpu.VMEM((STEPS, 8, 8, 128), f32),
            dma((3,)),
            dma((8,)),
            dma((8,)),
            dma((slots,)),
            dma((slots,)),
            dma((exchanges, 8)),
            dma((exchanges, 8)),
            dma((STEPS, 2, 8)),
            dma((STEPS, 2, 8)),
            dma((1,)),
            dma((1,)),
        ] + [pltpu.VMEM(wide, f32)] * 7 + [pltpu.VMEM((slots + 1, *wide), f32)]
        + [pltpu.VMEM((slots, *wide), f32)] * 3 + [pltpu.VMEM(wide, f32)] * (TERMS - 1),
        compiler_params=pltpu.CompilerParams(
            collective_id=0, has_side_effects=True, vmem_limit_bytes=56 * 1024 * 1024
        ),
    )(
        initial.reshape(NZ * NXL, NYL),
        capacity.reshape(NZ * NXL, NYL),
        profile.reshape(1, NZ),
        bore_loop,
        plan[0],
    )
    return out.reshape(1, NZ, NXL, NYL)


def solution(mesh):
    sizes = (mesh.shape["tm"], mesh.shape["gx"], mesh.shape["gy"])
    return jax.shard_map(
        functools.partial(per_device, sizes),
        mesh=mesh,
        in_specs=(
            P(None, "gx", "gy"),
            P(None, "gx", "gy"),
            P(),
            P("gx", "gy"),
            P("tm", None, None),
        ),
        out_specs=P("tm", None, "gx", "gy"),
        check_vma=False,
    )
```

```python
import functools

import jax
import jax.numpy as jnp
import numpy as np
from jax import lax
from jax.experimental import pallas as pl
from jax.experimental.pallas import tpu as pltpu
from jax.sharding import PartitionSpec as P

MESH = pl.DeviceIdType.MESH
STEPS = 2
TERMS = 8
LOOPS = 16
HORIZON = 4.0 / 3.0
EXPONENT = 16.0

NZ, NXL, NYL = 64, 8, 128
HALF = NXL // 2
REACH = TERMS - 1
OWN = REACH
WIDE = REACH + HALF
LAST = WIDE - 1
ROWS = NYL + 32
LOW, HIGH = 16, 16 + NYL
CHUNK = 16


def cheb_coeffs(term_count):
    angles = np.pi * (np.arange(term_count) + 0.5) / term_count
    cheb_nodes = np.cos(angles)
    samples = np.exp(-EXPONENT * (cheb_nodes + 1.0))
    coeffs = [
        2.0 / term_count * float(np.sum(samples * np.cos(term_index * angles)))
        for term_index in range(term_count)
    ]
    coeffs[0] = coeffs[0] / 2.0
    return coeffs


def chunks(low, high, size):
    return [(r, min(size, high - r)) for r in range(low, high, size)]


def kernel(
    sizes,
    init_hbm, cap_hbm, prof_ref, bore_ref, plan_ref, out_ref,
    nat, src, xbuf, hbuf, bext, plans, rates, mom, pay, coef, sums_x, sums_y,
    load_sem, bore_send, bore_recv, plan_send, plan_recv, halo_send, halo_recv,
    sum_send, sum_recv, shift_send, shift_recv, part_send, part_recv,
    heat, inv, dinv, u0, ku, ca, cg, xs, v0s, v1s, v2s, *ts,
):
    slices, nx, ny = sizes
    slots = max(1, slices // 2)
    inv_step = STEPS * slices / HORIZON
    tm, gx, gy = lax.axis_index("tm"), lax.axis_index("gx"), lax.axis_index("gy")
    f32 = jnp.float32
    cheb = cheb_coeffs(TERMS)

    def has(a, b):
        x, y = gx + a, gy + b
        return (x >= 0) & (x < nx) & (y >= 0) & (y < ny)

    around = [(a, b) for b in (-1, 0, 1) for a in (-1, 0, 1) if (a, b) != (0, 0)]
    around.sort(key=lambda ab: ab[1] == 0)

    load_cap = pltpu.make_async_copy(cap_hbm, nat.at[0], load_sem.at[0])
    load_init = pltpu.make_async_copy(init_hbm, nat.at[1], load_sem.at[1])
    load_cap.start()
    load_init.start()

    barrier = pltpu.get_barrier_semaphore()
    for d in range(1, nx):
        pl.semaphore_signal(barrier, inc=1, device_id={"gx": lax.rem(gx + d, nx)}, device_id_type=MESH)
    for d in range(1, ny):
        pl.semaphore_signal(barrier, inc=1, device_id={"gy": lax.rem(gy + d, ny)}, device_id_type=MESH)
    for a, b in around:
        if a and b:
            @pl.when(has(a, b))
            def _():
                pl.semaphore_signal(barrier, inc=1, device_id={"gx": gx + a, "gy": gy + b}, device_id_type=MESH)
    spans = [1] + [2 * s for s in range(1, slots)]
    for s in spans:
        @pl.when(tm >= s)
        def _():
            pl.semaphore_signal(barrier, inc=1, device_id={"tm": tm - s}, device_id_type=MESH)

    lane = lax.broadcasted_iota(jnp.int32, (8, 128), 1)

    def halo_copy(e, at, n, a, b, q=None):
        rows = pl.ds(LOW, NYL) if b == 0 else pl.ds(LOW, 8) if b < 0 else pl.ds(HIGH - 8, 8)
        lines, first = (HALF, 0) if q is None else (1, q)
        if a == 0:
            dst = hbuf.at[e, 1 if b < 0 else 0]
        else:
            at_rows = pl.ds(8, NYL) if b == 0 else pl.ds(8 + NYL, 8) if b < 0 else pl.ds(0, 8)
            dst = xbuf.at[e, 1 if a < 0 else 0, pl.ds(first, lines), at_rows, :]
        return pltpu.make_async_remote_copy(
            src_ref=at.at[pl.ds(OWN + first, lines), rows, :], dst_ref=dst,
            send_sem=halo_send.at[e, n] if q is None else part_send.at[q, n],
            recv_sem=halo_recv.at[e, n] if q is None else part_recv.at[q, n],
            device_id={"gx": gx + a, "gy": gy + b}, device_id_type=MESH,
        )

    def halo_start(e, at):
        for n, (a, b) in enumerate(around):
            @pl.when(has(a, b))
            def _():
                halo_copy(e, at, n, a, b).start()

    def halo_wait(e, at):
        for n, (a, b) in enumerate(around):
            @pl.when(has(-a, -b))
            def _():
                halo_copy(e, at, n, a, b).wait_recv()

    left, right, down, up = gx > 0, gx < nx - 1, gy > 0, gy < ny - 1

    low_lanes = lax.broadcasted_iota(jnp.int32, (1, 8, 128), 2) < NZ

    def halo_build(e, at):
        for r, n in [(0, 8), (8, NYL), (8 + NYL, 8)]:
            edge = down if r == 0 else up if r > 8 else True
            for crossed in (False, True):
                from_left = (~low_lanes if crossed else low_lanes) & left & edge
                from_right = (low_lanes if crossed else ~low_lanes) & right & edge
                for m in range(HALF - 1, REACH) if crossed else range(HALF - 1):
                    q = REACH - 1 - m if crossed else m + 1
                    one = xbuf[e, 0, q, r:r + n, :].reshape(n // 8, 8, 128)
                    two = xbuf[e, 1, q, r:r + n, :].reshape(n // 8, 8, 128)
                    value = jnp.where(from_left, one, jnp.where(from_right, two, f32(0.0)))
                    if crossed:
                        value = pltpu.roll(value, NZ, 2)
                    at[m, LOW - 8 + r:LOW - 8 + r + n, :] = value.reshape(n, 128)
        at[OWN:WIDE, LOW - 8:LOW, :] = jnp.where(down, hbuf[e, 0], f32(0.0))
        at[OWN:WIDE, HIGH:HIGH + 8, :] = jnp.where(up, hbuf[e, 1], f32(0.0))

    def to_wide(which, at):
        for q in range(HALF):
            top = nat[which, pl.ds(q, NZ, stride=NXL), :]
            low = nat[which, pl.ds(NXL - 1 - q, NZ, stride=NXL), :]
            at[OWN + q, LOW:HIGH, :] = jnp.concatenate([top, low], axis=0).T

    load_cap.wait()
    to_wide(0, heat)
    greeted = nx - 1 + ny - 1
    for a, b in around:
        if a and b:
            greeted = greeted + jnp.where(has(a, b), 1, 0)
    for s in spans:
        greeted = greeted + jnp.where(tm + s < slices, 1, 0)
    pl.semaphore_wait(barrier, greeted)
    plans[0] = jnp.zeros((8, 128), jnp.int32)
    plans[0, 0:STEPS, 0:LOOPS] = plan_ref[...]
    bext[1, 8:16, :] = bore_ref[...]
    for n, (a, b) in enumerate(around):
        @pl.when(has(a, b))
        def _():
            pltpu.make_async_remote_copy(
                src_ref=bore_ref, dst_ref=bext.at[1 - b, pl.ds(8 * (1 - a), 8), :],
                send_sem=bore_send.at[n], recv_sem=bore_recv.at[n],
                device_id={"gx": gx + a, "gy": gy + b}, device_id_type=MESH,
            ).start()
    for s in range(1, slots):
        @pl.when(tm + 2 * s < slices)
        def _():
            pltpu.make_async_remote_copy(
                src_ref=plans.at[0], dst_ref=plans.at[s],
                send_sem=plan_send.at[s], recv_sem=plan_recv.at[s],
                device_id={"tm": tm + 2 * s}, device_id_type=MESH,
            ).start()

    halo_start(0, heat)
    load_init.wait()
    to_wide(1, u0)
    halo_start(1, u0)

    for sy in range(3):
        for sx in range(3):
            if (sx, sy) != (1, 1):
                @pl.when(~has(sx - 1, sy - 1))
                def _():
                    bext[sy, 8 * sx:8 * sx + 8, :] = jnp.full((8, 128), LOOPS, jnp.int32)
    for n, (a, b) in enumerate(around):
        @pl.when(has(-a, -b))
        def _():
            pltpu.make_async_remote_copy(
                src_ref=bore_ref, dst_ref=bext.at[1 - b, pl.ds(8 * (1 - a), 8), :],
                send_sem=bore_send.at[n], recv_sem=bore_recv.at[n],
                device_id={"gx": gx - a, "gy": gy - b}, device_id_type=MESH,
            ).wait_recv()
    for s in range(1, slots):
        @pl.when(tm - 2 * s >= 0)
        def _():
            pltpu.make_async_remote_copy(
                src_ref=plans.at[0], dst_ref=plans.at[s],
                send_sem=plan_send.at[s], recv_sem=plan_recv.at[s],
                device_id={"tm": tm - 2 * s}, device_id_type=MESH,
            ).wait_recv()

        @pl.when(tm - 2 * s < 0)
        def _():
            plans[s] = plans[0]

    SPAN = NYL + 16
    loops = jnp.concatenate([bext[0], bext[1], bext[2]], axis=0)
    for s in range(slots):
        table = plans[s].astype(f32) - 3.5
        for n in range(STEPS):
            at_row = (s * STEPS + n) * SPAN
            rate = jnp.zeros((72, 128), f32)
            for v in range(LOOPS):
                rate = jnp.where(loops == v, jnp.broadcast_to(table[n:n + 1, v:v + 1], (72, 128)), rate)
            turned = jnp.concatenate([rate, jnp.zeros((56, 128), f32)], axis=0).T
            rates[at_row:at_row + 8, :] = pltpu.roll(turned[120:128, :], 24, 1)
            rates[at_row + 8:at_row + 8 + NYL, :] = turned
            rates[at_row + 8 + NYL:at_row + SPAN, :] = pltpu.roll(turned[0:8, :], 104, 1)
    depth = jnp.concatenate([prof_ref[...], prof_ref[...]], axis=1)

    def spread(m, _):
        here = 32 + m - REACH
        there = 32 + NXL - 1 - (m - REACH)
        pick_row = lax.broadcasted_iota(jnp.int32, (128, 128), 0)
        pick_lane = lax.broadcasted_iota(jnp.int32, (128, 128), 1)
        pick = jnp.where(pick_row == jnp.where(pick_lane < NZ, here, there), f32(1.0), f32(0.0)).astype(jnp.bfloat16)
        wide = jnp.dot(rates[...].astype(jnp.bfloat16), pick, preferred_element_type=f32)
        src[m] = wide * depth
        return _

    lax.fori_loop(1, WIDE, spread, 0)

    def rolled(value, by):
        return pltpu.roll(value, by, 2)

    def beside(at, first, r, n):
        count = WIDE - first
        mid = at[first:WIDE, r:r + n, :]
        before = jnp.concatenate([at[first - 1:first, r:r + n, :], mid[:-1]], axis=0) if count > 1 else at[first - 1:first, r:r + n, :]
        across = rolled(mid[-1:], NZ)
        after = jnp.concatenate([mid[1:], across], axis=0) if count > 1 else across
        cols = at[first:WIDE, r - 1:r - 1 + n, :] + at[first:WIDE, r + 1:r + 1 + n, :]
        z_lane = lax.broadcasted_iota(jnp.int32, (count, n, 128), 2) & (NZ - 1)
        above = jnp.where(z_lane != 0, rolled(mid, 1), f32(0.0))
        below = jnp.where(z_lane != NZ - 1, rolled(mid, 127), f32(0.0))
        return mid, ((before + after) + cols) + (above + below)

    def blocks(first, wide):
        return chunks(LOW - 8, HIGH + 8, CHUNK) if wide else chunks(LOW, HIGH, CHUNK)

    def add_own(total, value, first, r, n):
        value = value[OWN - first:]
        low, high = max(LOW - r, 0), min(HIGH - r, n)
        if high <= low:
            return total
        value = value[:, low:high, :]
        return total + jnp.sum(value.reshape(-1, 8, 128), axis=0)

    halo_wait(0, heat)
    halo_build(0, heat)

    for r, n in chunks(LOW - 8, HIGH + 8, CHUNK):
        cap = heat[:, r:r + n, :]
        inside = cap > 0.0
        dinv[:, r:r + n, :] = jnp.where(inside, 1.0 / (cap * f32(inv_step) + 6.0), f32(0.0))
        inv[:, r:r + n, :] = jnp.where(inside, 1.0 / cap, f32(0.0))

    halo_wait(1, u0)
    halo_build(1, u0)
    for r, n in blocks(1, True):
        mid, total = beside(u0, 1, r, n)
        ku[1:WIDE, r:r + n, :] = 6.0 * mid - total

    zero = jnp.zeros((8, 128), f32)
    early, late = list(range(slots - 1, slots // 2 - 1, -1)), list(range(slots // 2 - 1, -1, -1))
    group_of = {s: g for g, group in enumerate((early, late)) for s in group}

    def krylov(n_step, s, first):
        x, v0, v1, v2 = xs.at[s], v0s.at[s], v1s.at[s], v2s.at[s]
        flag = jnp.where(tm - 2 * s == 0, f32(1.0), f32(0.0))
        base = s * (STEPS * SPAN) + n_step * SPAN
        sums = [zero] * 6
        for r, n in blocks(first, True):
            residual = src[first:WIDE, pl.ds(pl.multiple_of(base + (r - 8), 8), n), :]
            if n_step == 0:
                residual = residual - flag * ku[first:WIDE, r:r + n, :]
            else:
                mid, total = beside(x, first, r, n)
                residual = residual - (6.0 * mid - total)
            z = dinv[first:WIDE, r:r + n, :] * residual
            v0[first:WIDE, r:r + n, :] = z
            sums[0] = add_own(sums[0], residual * z, first, r, n)
        for k, (now, then) in enumerate(((v0, v1), (v1, v2))):
            begin = first + 1 + k
            for r, n in blocks(begin, True):
                mid, total = beside(now, begin, r, n)
                z = dinv[begin:WIDE, r:r + n, :] * total
                then[begin:WIDE, r:r + n, :] = z
                sums[2 * k + 1] = add_own(sums[2 * k + 1], mid * total, begin, r, n)
                sums[2 * k + 2] = add_own(sums[2 * k + 2], z * total, begin, r, n)
        for r, n in blocks(OWN, False):
            mid, total = beside(v2, OWN, r, n)
            sums[5] = add_own(sums[5], mid * total, OWN, r, n)
        for j, total in enumerate(sums):
            mom[n_step, group_of[s], j, s:s + 1, :] = jnp.sum(total, axis=0, keepdims=True)

    stages = (("gx", nx, gx, sums_x), ("gy", ny, gy, sums_y))

    def sum_copy(n_step, g, stage, d):
        axis, count, me, buf = stages[stage]
        return pltpu.make_async_remote_copy(
            src_ref=pay.at[n_step, g, stage], dst_ref=buf.at[n_step, g, d],
            send_sem=sum_send.at[n_step, g, stage, d], recv_sem=sum_recv.at[n_step, g, stage, d],
            device_id={axis: lax.rem(me + d, count)}, device_id_type=MESH,
        )

    def sum_send_all(n_step, g, stage):
        for d in range(1, stages[stage][1]):
            sum_copy(n_step, g, stage, d).start()

    def sum_collect(n_step, g, stage):
        for d in range(1, stages[stage][1]):
            sum_copy(n_step, g, stage, d).wait_recv()
        total = pay[n_step, g, stage]
        for d in range(1, stages[stage][1]):
            total = total + stages[stage][3][n_step, g, d]
        return total

    def sum_start(n_step, g):
        packed = jnp.zeros((8, 128), f32)
        for j in range(6):
            packed = jnp.where(lane == j, jnp.sum(mom[n_step, g, j], axis=1, keepdims=True), packed)
        pay[n_step, g, 0] = packed
        sum_send_all(n_step, g, 0)

    def sum_turn(n_step, g):
        pay[n_step, g, 1] = sum_collect(n_step, g, 0)
        sum_send_all(n_step, g, 1)

    def sum_finish(n_step, g):
        total = sum_collect(n_step, g, 1)
        weights = cg_coefficients([jnp.broadcast_to(total[:, j:j + 1], (8, 128)) for j in range(6)])
        for i in range(3):
            coef[n_step, g, i] = weights[i]
        for stage in range(2):
            for d in range(1, stages[stage][1]):
                sum_copy(n_step, g, stage, d).wait_send()

    def cg_coefficients(mu):
        def inner(p, q, m):
            total = None
            for i, a in enumerate(p):
                for j, b in enumerate(q):
                    term = a * b * m[i + j]
                    total = term if total is None else total + term
            return total

        gap = [mu[j] - mu[j + 1] for j in range(5)]
        one = jnp.ones((8, 128), f32)
        x = [jnp.zeros((8, 128), f32)] * 3
        z, direction = [one], [one]
        inner_now = mu[0]
        for it in range(3):
            step = inner_now / inner(direction, direction, gap)
            x = [x[i] + step * direction[i] if i < len(direction) else x[i] for i in range(3)]
            if it < 2:
                grown = direction + [jnp.zeros((8, 128), f32)]
                shifted = [jnp.zeros((8, 128), f32)] + direction
                z = [(z[i] if i < len(z) else 0.0) - step * (grown[i] - shifted[i]) for i in range(len(grown))]
                inner_next = inner(z, z, mu)
                ratio = inner_next / inner_now
                direction = [z[i] + ratio * direction[i] if i < len(direction) else z[i] for i in range(len(z))]
                inner_now = inner_next
        return x

    def update(n_step, s):
        w = [coef[n_step, group_of[s], i, s:s + 1, :].reshape(1, 1, 128) for i in range(3)]
        flag = jnp.where(tm - 2 * s == 0, f32(1.0), f32(0.0))
        begin = 3 if n_step == 0 else OWN
        for r, n in blocks(begin, n_step == 0):
            here = (s, slice(begin, WIDE), slice(r, r + n))
            value = w[0] * v0s[here] + w[1] * v1s[here] + w[2] * v2s[here]
            if n_step == 0:
                xs[here] = value + flag * u0[begin:WIDE, r:r + n, :]
            else:
                xs[here] = jnp.where(tm - 2 * s >= 0, value + xs[here], f32(0.0))

    def solve(n_step, group, between=None):
        for i, s in enumerate(group):
            if i == len(group) - 1 and between is not None:
                between()
            krylov(n_step, s, (1, 4)[n_step])

    mom[...] = jnp.zeros(mom.shape, f32)
    solve(0, early)
    sum_start(0, 0)
    if late:
        solve(0, late, lambda: sum_turn(0, 0))
        sum_start(0, 1)
    else:
        sum_turn(0, 0)
    sum_finish(0, 0)
    for s in early:
        update(0, s)
    solve(1, early, (lambda: sum_turn(0, 1)) if late else None)
    sum_start(1, 0)
    if late:
        sum_finish(0, 1)
        for s in late:
            update(0, s)
        solve(1, late, lambda: sum_turn(1, 0))
        sum_start(1, 1)
    else:
        sum_turn(1, 0)
    sum_finish(1, 0)
    for s in early:
        update(1, s)

    plan_rows = []
    span = slots // 2
    while span >= 1:
        for s in range(2 * span - 1, span - 1, -1):
            plan_rows.append((s, s - span, 2 * span))
        span //= 2
    plan_rows.append((slots, 0, 1))
    order = [row[0] for row in plan_rows]
    last = len(plan_rows) - 1
    finished = {s: max((p for p, row in enumerate(plan_rows) if row[1] == s), default=-1) for s in order[:-1]}

    def pick(p, values):
        out = values[-1]
        for i in range(len(values) - 2, -1, -1):
            out = jnp.where(p == i, values[i], out)
        return out

    def shift(q):
        return pltpu.make_async_remote_copy(
            src_ref=xs.at[0, pl.ds(OWN + q, 1), pl.ds(LOW, NYL), :],
            dst_ref=xs.at[slots, pl.ds(OWN + q, 1), pl.ds(LOW, NYL), :],
            send_sem=shift_send.at[q], recv_sem=shift_recv.at[q],
            device_id={"tm": lax.rem(tm + 1, slices)}, device_id_type=MESH,
        )

    across = [(n, a) for n, (a, b) in enumerate(around) if b == 0]

    def pass_on():
        state = xs.at[slots]

        @pl.when(tm < slices - 1)
        def _():
            for q in range(HALF):
                shift(q).start()

        @pl.when(tm == 0)
        def _():
            xs[slots, OWN:WIDE, LOW:HIGH, :] = jnp.zeros((HALF, NYL, 128), f32)

        for q in range(HALF):
            @pl.when(tm > 0)
            def _():
                shift(q).wait_recv()

            for n, a in across:
                @pl.when(has(a, 0))
                def _():
                    halo_copy(2 + last, state, n, a, 0, q).start()
        for n, (a, b) in enumerate(around):
            if b != 0:
                @pl.when(has(a, b))
                def _():
                    halo_copy(2 + last, state, n, a, b).start()

        @pl.when(tm < slices - 1)
        def _():
            for q in range(HALF):
                shift(q).wait_send()

    waiting = [s for s in order[:-1] if finished[s] < 0]
    if waiting:
        halo_start(2 + order.index(waiting[0]), xs.at[waiting[0]])
    if late:
        sum_turn(1, 1)
    for s in waiting[1:]:
        halo_start(2 + order.index(s), xs.at[s])
    if late:
        sum_finish(1, 1)
        for s in late:
            update(1, s)
    if last == 0:
        pass_on()

    def combine(before, now, first, r, n):
        mid, total = beside(now, first, r, n)
        return mid, cg[first:WIDE, r:r + n, :] * mid - ca[first:WIDE, r:r + n, :] * total, before[first:WIDE, r:r + n, :] if before is not None else None

    def section(p, carry):
        at, to = pick(p, order), pick(p, [row[1] for row in plan_rows])
        factor = pick(p, [jnp.float32(2.0 * row[2] / (12.0 * slices)) for row in plan_rows])
        for r, n in chunks(LOW - 8, HIGH + 8, CHUNK):
            a = inv[:, r:r + n, :] * factor
            ca[:, r:r + n, :] = a
            cg[:, r:r + n, :] = 6.0 * a - 2.0
        ts[0][OWN:WIDE, LOW:HIGH, :] = xs[at, OWN:WIDE, LOW:HIGH, :]
        for n, (a, b) in enumerate(around):
            if b != 0:
                @pl.when(has(-a, -b))
                def _():
                    halo_copy(2 + p, xs.at[at], n, a, b).wait_recv()
            else:
                @pl.when(has(-a, -b) & (p < last))
                def _():
                    halo_copy(2 + p, xs.at[at], n, a, b).wait_recv()

                @pl.when(has(-a, -b) & (p == last))
                def _():
                    for q in range(HALF):
                        halo_copy(2 + p, xs.at[at], n, a, b, q).wait_recv()
        halo_build(2 + p, ts[0])
        for j in range(1, TERMS - 1):
            for r, n in blocks(j, True):
                mid, value, before = combine(ts[j - 2] if j > 1 else None, ts[j - 1], j, r, n)
                ts[j][j:WIDE, r:r + n, :] = 0.5 * value if j == 1 else value - before
        for r, n in blocks(OWN, False):
            mid, value, before = combine(ts[5], ts[6], OWN, r, n)
            value = f32(cheb[7]) * (value - before) + f32(cheb[6]) * mid + f32(cheb[5]) * before
            for j in range(5):
                value = value + f32(cheb[j]) * ts[j][OWN:WIDE, r:r + n, :]
            xs[to, OWN:WIDE, r:r + n, :] = xs[to, OWN:WIDE, r:r + n, :] + value
        for s, p_done in finished.items():
            if p_done >= 0:
                @pl.when(p == p_done)
                def _():
                    halo_start(2 + order.index(s), xs.at[s])
        if last > 0:
            @pl.when(p == last - 1)
            def _():
                pass_on()
        return carry

    lax.fori_loop(0, last + 1, section, 0)

    for q in range(HALF):
        turned = xs[0, OWN + q, LOW:HIGH, :].T
        nat[1, pl.ds(q, NZ, stride=NXL), :] = turned[0:NZ, :]
        nat[1, pl.ds(NXL - 1 - q, NZ, stride=NXL), :] = turned[NZ:2 * NZ, :]
    store_out = pltpu.make_async_copy(nat.at[1], out_ref, load_sem.at[2])
    store_out.start()

    for n, (a, b) in enumerate(around):
        @pl.when(has(a, b))
        def _():
            pltpu.make_async_remote_copy(
                src_ref=bore_ref, dst_ref=bext.at[1 - b, pl.ds(8 * (1 - a), 8), :],
                send_sem=bore_send.at[n], recv_sem=bore_recv.at[n],
                device_id={"gx": gx + a, "gy": gy + b}, device_id_type=MESH,
            ).wait_send()
            halo_copy(0, heat, n, a, b).wait_send()
            halo_copy(1, u0, n, a, b).wait_send()
            for p, s in enumerate(order):
                if p == last and b == 0:
                    for q in range(HALF):
                        halo_copy(2 + p, xs.at[s], n, a, b, q).wait_send()
                else:
                    halo_copy(2 + p, xs.at[s], n, a, b).wait_send()
    for s in range(1, slots):
        @pl.when(tm + 2 * s < slices)
        def _():
            pltpu.make_async_remote_copy(
                src_ref=plans.at[0], dst_ref=plans.at[s],
                send_sem=plan_send.at[s], recv_sem=plan_recv.at[s],
                device_id={"tm": tm + 2 * s}, device_id_type=MESH,
            ).wait_send()
    store_out.wait()


def per_device(sizes, initial, capacity, profile, bore_loop, plan):
    slices = sizes[0]
    slots = max(1, slices // 2)
    exchanges = 2 + (slots - 1) + 1
    wide = (WIDE, ROWS, 128)
    f32 = jnp.float32
    dma = pltpu.SemaphoreType.DMA
    out = pl.pallas_call(
        functools.partial(kernel, sizes),
        out_shape=jax.ShapeDtypeStruct((NZ * NXL, NYL), f32),
        in_specs=[
            pl.BlockSpec(memory_space=pl.ANY),
            pl.BlockSpec(memory_space=pl.ANY),
            pl.BlockSpec(memory_space=pltpu.VMEM),
            pl.BlockSpec(memory_space=pltpu.VMEM),
            pl.BlockSpec(memory_space=pltpu.VMEM),
        ],
        out_specs=pl.BlockSpec(memory_space=pl.ANY),
        scratch_shapes=[
            pltpu.VMEM((2, NZ * NXL, NYL), f32),
            pltpu.VMEM((WIDE, slots * STEPS * (NYL + 16), 128), f32),
            pltpu.VMEM((exchanges, 2, HALF, NYL + 16, 128), f32),
            pltpu.VMEM((exchanges, 2, HALF, 8, 128), f32),
            pltpu.VMEM((3, 24, 128), jnp.int32),
            pltpu.VMEM((slots, 8, 128), jnp.int32),
            pltpu.VMEM((slots * STEPS * (NYL + 16), 128), f32),
            pltpu.VMEM((STEPS, 2, 6, 8, 128), f32),
            pltpu.VMEM((STEPS, 2, 2, 8, 128), f32),
            pltpu.VMEM((STEPS, 2, 3, 8, 128), f32),
            pltpu.VMEM((STEPS, 2, 8, 8, 128), f32),
            pltpu.VMEM((STEPS, 2, 8, 8, 128), f32),
            dma((3,)),
            dma((8,)),
            dma((8,)),
            dma((slots,)),
            dma((slots,)),
            dma((exchanges, 8)),
            dma((exchanges, 8)),
            dma((STEPS, 2, 2, 8)),
            dma((STEPS, 2, 2, 8)),
            dma((HALF,)),
            dma((HALF,)),
            dma((HALF, 8)),
            dma((HALF, 8)),
        ] + [pltpu.VMEM(wide, f32)] * 7 + [pltpu.VMEM((slots + 1, *wide), f32)]
        + [pltpu.VMEM((slots, *wide), f32)] * 3 + [pltpu.VMEM(wide, f32)] * (TERMS - 1),
        compiler_params=pltpu.CompilerParams(
            collective_id=0, has_side_effects=True, vmem_limit_bytes=56 * 1024 * 1024
        ),
    )(
        initial.reshape(NZ * NXL, NYL),
        capacity.reshape(NZ * NXL, NYL),
        profile.reshape(1, NZ),
        bore_loop,
        plan[0],
    )
    return out.reshape(1, NZ, NXL, NYL)


def solution(mesh):
    sizes = (mesh.shape["tm"], mesh.shape["gx"], mesh.shape["gy"])
    return jax.shard_map(
        functools.partial(per_device, sizes),
        mesh=mesh,
        in_specs=(
            P(None, "gx", "gy"),
            P(None, "gx", "gy"),
            P(),
            P("gx", "gy"),
            P("tm", None, None),
        ),
        out_specs=P("tm", None, "gx", "gy"),
        check_vma=False,
    )
```

```python
import functools

import jax
import jax.numpy as jnp
import numpy as np
from jax import lax
from jax.experimental import pallas as pl
from jax.experimental.pallas import tpu as pltpu
from jax.sharding import PartitionSpec as P

MESH = pl.DeviceIdType.MESH
STEPS = 2
TERMS = 8
LOOPS = 16
HORIZON = 4.0 / 3.0
EXPONENT = 16.0

NZ, NXL, NYL = 64, 8, 128
HALF = NXL // 2
REACH = TERMS - 1
OWN = REACH
WIDE = REACH + HALF
LAST = WIDE - 1
ROWS = NYL + 32
LOW, HIGH = 16, 16 + NYL
CHUNK = 16
MID = LOW + NYL // 2
PARTS = ((LOW, NYL // 2), (MID, 8), (MID + 8, NYL // 2 - 8))


def cheb_coeffs(term_count):
    angles = np.pi * (np.arange(term_count) + 0.5) / term_count
    cheb_nodes = np.cos(angles)
    samples = np.exp(-EXPONENT * (cheb_nodes + 1.0))
    coeffs = [
        2.0 / term_count * float(np.sum(samples * np.cos(term_index * angles)))
        for term_index in range(term_count)
    ]
    coeffs[0] = coeffs[0] / 2.0
    return coeffs


def chunks(low, high, size):
    return [(r, min(size, high - r)) for r in range(low, high, size)]


def kernel(
    sizes,
    init_hbm, cap_hbm, prof_ref, bore_ref, plan_ref, out_ref,
    nat, src, xbuf, hbuf, bext, plans, rates, mom, pay, coef, sums_x, sums_y,
    load_sem, bore_send, bore_recv, plan_send, plan_recv, halo_send, halo_recv,
    sum_send, sum_recv, shift_send, shift_recv, part_send, part_recv,
    heat, inv, dinv, u0, ku, ca, cg, xs, v0s, v1s, v2s, *ts,
):
    slices, nx, ny = sizes
    slots = max(1, slices // 2)
    inv_step = STEPS * slices / HORIZON
    tm, gx, gy = lax.axis_index("tm"), lax.axis_index("gx"), lax.axis_index("gy")
    f32 = jnp.float32
    cheb = cheb_coeffs(TERMS)

    def has(a, b):
        x, y = gx + a, gy + b
        return (x >= 0) & (x < nx) & (y >= 0) & (y < ny)

    around = [(a, b) for b in (-1, 0, 1) for a in (-1, 0, 1) if (a, b) != (0, 0)]
    around.sort(key=lambda ab: ab[1] == 0)

    load_cap = pltpu.make_async_copy(cap_hbm, nat.at[0], load_sem.at[0])
    load_init = pltpu.make_async_copy(init_hbm, nat.at[1], load_sem.at[1])
    load_cap.start()
    load_init.start()

    barrier = pltpu.get_barrier_semaphore()
    for d in range(1, nx):
        pl.semaphore_signal(barrier, inc=1, device_id={"gx": lax.rem(gx + d, nx)}, device_id_type=MESH)
    for d in range(1, ny):
        pl.semaphore_signal(barrier, inc=1, device_id={"gy": lax.rem(gy + d, ny)}, device_id_type=MESH)
    for a, b in around:
        if a and b:
            @pl.when(has(a, b))
            def _():
                pl.semaphore_signal(barrier, inc=1, device_id={"gx": gx + a, "gy": gy + b}, device_id_type=MESH)
    spans = [1] + [2 * s for s in range(1, slots)]
    for s in spans:
        @pl.when(tm >= s)
        def _():
            pl.semaphore_signal(barrier, inc=1, device_id={"tm": tm - s}, device_id_type=MESH)

    lane = lax.broadcasted_iota(jnp.int32, (8, 128), 1)

    def halo_copy(e, at, n, a, b, q=None):
        first, size = (LOW, NYL) if q is None else PARTS[q]
        rows = pl.ds(first, size) if b == 0 else pl.ds(LOW, 8) if b < 0 else pl.ds(HIGH - 8, 8)
        if a == 0:
            dst = hbuf.at[e, 1 if b < 0 else 0]
        else:
            at_rows = pl.ds(first - LOW + 8, size) if b == 0 else pl.ds(8 + NYL, 8) if b < 0 else pl.ds(0, 8)
            dst = xbuf.at[e, 1 if a < 0 else 0, :, at_rows, :]
        return pltpu.make_async_remote_copy(
            src_ref=at.at[pl.ds(OWN, HALF), rows, :], dst_ref=dst,
            send_sem=halo_send.at[e, n] if q is None else part_send.at[e, q, n],
            recv_sem=halo_recv.at[e, n] if q is None else part_recv.at[e, q, n],
            device_id={"gx": gx + a, "gy": gy + b}, device_id_type=MESH,
        )

    def parts_start(e, at, parts, sides):
        for n, (a, b) in enumerate(around):
            if b in sides:
                @pl.when(has(a, b))
                def _():
                    halo_copy(e, at, n, a, b).start()
        for q in parts:
            for n, (a, b) in enumerate(around):
                if b == 0:
                    @pl.when(has(a, b))
                    def _():
                        halo_copy(e, at, n, a, b, q).start()

    def parts_wait(e, at, parts, side):
        for n, (a, b) in enumerate(around):
            if b == side or b == 0:
                @pl.when(has(-a, -b))
                def _():
                    if b == 0:
                        for q in parts:
                            halo_copy(e, at, n, a, b, q).wait_recv()
                    else:
                        halo_copy(e, at, n, a, b).wait_recv()

    def halo_start(e, at):
        for n, (a, b) in enumerate(around):
            @pl.when(has(a, b))
            def _():
                halo_copy(e, at, n, a, b).start()

    def halo_wait(e, at):
        for n, (a, b) in enumerate(around):
            @pl.when(has(-a, -b))
            def _():
                halo_copy(e, at, n, a, b).wait_recv()

    left, right, down, up = gx > 0, gx < nx - 1, gy > 0, gy < ny - 1

    low_lanes = lax.broadcasted_iota(jnp.int32, (1, 8, 128), 2) < NZ

    def halo_build(e, at, segments=((0, 8), (8, NYL), (8 + NYL, 8))):
        for r, n in segments:
            edge = down if r == 0 else up if r == 8 + NYL else True
            for crossed in (False, True):
                from_left = (~low_lanes if crossed else low_lanes) & left & edge
                from_right = (low_lanes if crossed else ~low_lanes) & right & edge
                for m in range(HALF - 1, REACH) if crossed else range(HALF - 1):
                    q = REACH - 1 - m if crossed else m + 1
                    one = xbuf[e, 0, q, r:r + n, :].reshape(n // 8, 8, 128)
                    two = xbuf[e, 1, q, r:r + n, :].reshape(n // 8, 8, 128)
                    value = jnp.where(from_left, one, jnp.where(from_right, two, f32(0.0)))
                    if crossed:
                        value = pltpu.roll(value, NZ, 2)
                    at[m, LOW - 8 + r:LOW - 8 + r + n, :] = value.reshape(n, 128)
        if (0, 8) in segments:
            at[OWN:WIDE, LOW - 8:LOW, :] = jnp.where(down, hbuf[e, 0], f32(0.0))
        if (8 + NYL, 8) in segments:
            at[OWN:WIDE, HIGH:HIGH + 8, :] = jnp.where(up, hbuf[e, 1], f32(0.0))

    def to_wide(which, at):
        for q in range(HALF):
            top = nat[which, pl.ds(q, NZ, stride=NXL), :]
            low = nat[which, pl.ds(NXL - 1 - q, NZ, stride=NXL), :]
            at[OWN + q, LOW:HIGH, :] = jnp.concatenate([top, low], axis=0).T

    greeted = nx - 1 + ny - 1
    for a, b in around:
        if a and b:
            greeted = greeted + jnp.where(has(a, b), 1, 0)
    for s in spans:
        greeted = greeted + jnp.where(tm + s < slices, 1, 0)
    pl.semaphore_wait(barrier, greeted)
    plans[0] = jnp.zeros((8, 128), jnp.int32)
    plans[0, 0:STEPS, 0:LOOPS] = plan_ref[...]
    bext[1, 8:16, :] = bore_ref[...]
    for n, (a, b) in enumerate(around):
        @pl.when(has(a, b))
        def _():
            pltpu.make_async_remote_copy(
                src_ref=bore_ref, dst_ref=bext.at[1 - b, pl.ds(8 * (1 - a), 8), :],
                send_sem=bore_send.at[n], recv_sem=bore_recv.at[n],
                device_id={"gx": gx + a, "gy": gy + b}, device_id_type=MESH,
            ).start()
    for s in range(1, slots):
        @pl.when(tm + 2 * s < slices)
        def _():
            pltpu.make_async_remote_copy(
                src_ref=plans.at[0], dst_ref=plans.at[s],
                send_sem=plan_send.at[s], recv_sem=plan_recv.at[s],
                device_id={"tm": tm + 2 * s}, device_id_type=MESH,
            ).start()

    load_cap.wait()
    to_wide(0, heat)
    halo_start(0, heat)
    load_init.wait()
    to_wide(1, u0)
    halo_start(1, u0)

    for sy in range(3):
        for sx in range(3):
            if (sx, sy) != (1, 1):
                @pl.when(~has(sx - 1, sy - 1))
                def _():
                    bext[sy, 8 * sx:8 * sx + 8, :] = jnp.full((8, 128), LOOPS, jnp.int32)
    for n, (a, b) in enumerate(around):
        @pl.when(has(-a, -b))
        def _():
            pltpu.make_async_remote_copy(
                src_ref=bore_ref, dst_ref=bext.at[1 - b, pl.ds(8 * (1 - a), 8), :],
                send_sem=bore_send.at[n], recv_sem=bore_recv.at[n],
                device_id={"gx": gx - a, "gy": gy - b}, device_id_type=MESH,
            ).wait_recv()
    for s in range(1, slots):
        @pl.when(tm - 2 * s >= 0)
        def _():
            pltpu.make_async_remote_copy(
                src_ref=plans.at[0], dst_ref=plans.at[s],
                send_sem=plan_send.at[s], recv_sem=plan_recv.at[s],
                device_id={"tm": tm - 2 * s}, device_id_type=MESH,
            ).wait_recv()

        @pl.when(tm - 2 * s < 0)
        def _():
            plans[s] = plans[0]

    SPAN = NYL + 16
    loops = jnp.concatenate([bext[0], bext[1], bext[2]], axis=0)
    depth = jnp.concatenate([prof_ref[...], prof_ref[...]], axis=1)

    def sources(n_step, first):
        for s in range(slots):
            table = plans[s].astype(f32) - 3.5
            rate = jnp.zeros((72, 128), f32)
            for v in range(LOOPS):
                rate = jnp.where(loops == v, jnp.broadcast_to(table[n_step:n_step + 1, v:v + 1], (72, 128)), rate)
            turned = jnp.concatenate([rate, jnp.zeros((56, 128), f32)], axis=0).T
            at_row = s * SPAN
            rates[at_row:at_row + 8, :] = pltpu.roll(turned[120:128, :], 24, 1)
            rates[at_row + 8:at_row + 8 + NYL, :] = turned
            rates[at_row + 8 + NYL:at_row + SPAN, :] = pltpu.roll(turned[0:8, :], 104, 1)
        all_rates = rates[...].astype(jnp.bfloat16)

        def spread(m, carry):
            here = 32 + m - REACH
            there = 32 + NXL - 1 - (m - REACH)
            pick_row = lax.broadcasted_iota(jnp.int32, (128, 128), 0)
            pick_lane = lax.broadcasted_iota(jnp.int32, (128, 128), 1)
            pick = jnp.where(pick_row == jnp.where(pick_lane < NZ, here, there), f32(1.0), f32(0.0)).astype(jnp.bfloat16)
            wide = jnp.dot(all_rates, pick, preferred_element_type=f32)
            src[n_step, m] = wide * depth
            return carry

        lax.fori_loop(first, WIDE, spread, 0)

    sources(0, 1)

    def rolled(value, by):
        return pltpu.roll(value, by, 2)

    def beside(at, first, r, n):
        count = WIDE - first
        mid = at[first:WIDE, r:r + n, :]
        before = jnp.concatenate([at[first - 1:first, r:r + n, :], mid[:-1]], axis=0) if count > 1 else at[first - 1:first, r:r + n, :]
        across = rolled(mid[-1:], NZ)
        after = jnp.concatenate([mid[1:], across], axis=0) if count > 1 else across
        cols = at[first:WIDE, r - 1:r - 1 + n, :] + at[first:WIDE, r + 1:r + 1 + n, :]
        z_lane = lax.broadcasted_iota(jnp.int32, (count, n, 128), 2) & (NZ - 1)
        above = jnp.where(z_lane != 0, rolled(mid, 1), f32(0.0))
        below = jnp.where(z_lane != NZ - 1, rolled(mid, 127), f32(0.0))
        return mid, ((before + after) + cols) + (above + below)

    def blocks(first, wide):
        return chunks(LOW - 8, HIGH + 8, CHUNK) if wide else chunks(LOW, HIGH, CHUNK)

    def add_own(total, value, first, r, n):
        value = value[OWN - first:]
        low, high = max(LOW - r, 0), min(HIGH - r, n)
        if high <= low:
            return total
        value = value[:, low:high, :]
        return total + jnp.sum(value.reshape(-1, 8, 128), axis=0)

    halo_wait(0, heat)
    halo_build(0, heat)

    for r, n in chunks(LOW - 8, HIGH + 8, CHUNK):
        cap = heat[:, r:r + n, :]
        inside = cap > 0.0
        dinv[:, r:r + n, :] = jnp.where(inside, 1.0 / (cap * f32(inv_step) + 6.0), f32(0.0))
        inv[:, r:r + n, :] = jnp.where(inside, 1.0 / cap, f32(0.0))

    halo_wait(1, u0)
    halo_build(1, u0)
    for r, n in blocks(1, True):
        mid, total = beside(u0, 1, r, n)
        ku[1:WIDE, r:r + n, :] = 6.0 * mid - total

    zero = jnp.zeros((8, 128), f32)
    early, late = list(range(slots - 1, slots // 2 - 1, -1)), list(range(slots // 2 - 1, -1, -1))
    group_of = {s: g for g, group in enumerate((early, late)) for s in group}

    def krylov(n_step, s, first):
        x, v0, v1, v2 = xs.at[s], v0s.at[s], v1s.at[s], v2s.at[s]
        flag = jnp.where(tm - 2 * s == 0, f32(1.0), f32(0.0))
        base = s * SPAN
        sums = [zero] * 6
        for r, n in blocks(first, True):
            residual = src[n_step, first:WIDE, base + (r - 8):base + (r - 8) + n, :]
            if n_step == 0:
                residual = residual - flag * ku[first:WIDE, r:r + n, :]
            else:
                mid, total = beside(x, first, r, n)
                residual = residual - (6.0 * mid - total)
            z = dinv[first:WIDE, r:r + n, :] * residual
            v0[first:WIDE, r:r + n, :] = z
            sums[0] = add_own(sums[0], residual * z, first, r, n)
        for k, (now, then) in enumerate(((v0, v1), (v1, v2))):
            begin = first + 1 + k
            for r, n in blocks(begin, True):
                mid, total = beside(now, begin, r, n)
                z = dinv[begin:WIDE, r:r + n, :] * total
                then[begin:WIDE, r:r + n, :] = z
                sums[2 * k + 1] = add_own(sums[2 * k + 1], mid * total, begin, r, n)
                sums[2 * k + 2] = add_own(sums[2 * k + 2], z * total, begin, r, n)
        for r, n in blocks(OWN, False):
            mid, total = beside(v2, OWN, r, n)
            sums[5] = add_own(sums[5], mid * total, OWN, r, n)
        for j, total in enumerate(sums):
            mom[n_step, group_of[s], j, s:s + 1, :] = jnp.sum(total, axis=0, keepdims=True)

    stages = (("gx", nx, gx, sums_x), ("gy", ny, gy, sums_y))

    def sum_copy(n_step, g, stage, d):
        axis, count, me, buf = stages[stage]
        return pltpu.make_async_remote_copy(
            src_ref=pay.at[n_step, g, stage], dst_ref=buf.at[n_step, g, d],
            send_sem=sum_send.at[n_step, g, stage, d], recv_sem=sum_recv.at[n_step, g, stage, d],
            device_id={axis: lax.rem(me + d, count)}, device_id_type=MESH,
        )

    def sum_send_all(n_step, g, stage):
        for d in range(1, stages[stage][1]):
            sum_copy(n_step, g, stage, d).start()

    def sum_collect(n_step, g, stage):
        for d in range(1, stages[stage][1]):
            sum_copy(n_step, g, stage, d).wait_recv()
        total = pay[n_step, g, stage]
        for d in range(1, stages[stage][1]):
            total = total + stages[stage][3][n_step, g, d]
        return total

    def sum_start(n_step, g):
        packed = jnp.zeros((8, 128), f32)
        for j in range(6):
            packed = jnp.where(lane == j, jnp.sum(mom[n_step, g, j], axis=1, keepdims=True), packed)
        pay[n_step, g, 0] = packed
        sum_send_all(n_step, g, 0)

    def sum_turn(n_step, g):
        pay[n_step, g, 1] = sum_collect(n_step, g, 0)
        sum_send_all(n_step, g, 1)

    def sum_finish(n_step, g):
        total = sum_collect(n_step, g, 1)
        weights = cg_coefficients([jnp.broadcast_to(total[:, j:j + 1], (8, 128)) for j in range(6)])
        for i in range(3):
            coef[n_step, g, i] = weights[i]
        for stage in range(2):
            for d in range(1, stages[stage][1]):
                sum_copy(n_step, g, stage, d).wait_send()

    def cg_coefficients(mu):
        def inner(p, q, m):
            total = None
            for i, a in enumerate(p):
                for j, b in enumerate(q):
                    term = a * b * m[i + j]
                    total = term if total is None else total + term
            return total

        gap = [mu[j] - mu[j + 1] for j in range(5)]
        one = jnp.ones((8, 128), f32)
        x = [jnp.zeros((8, 128), f32)] * 3
        z, direction = [one], [one]
        inner_now = mu[0]
        for it in range(3):
            step = inner_now / inner(direction, direction, gap)
            x = [x[i] + step * direction[i] if i < len(direction) else x[i] for i in range(3)]
            if it < 2:
                grown = direction + [jnp.zeros((8, 128), f32)]
                shifted = [jnp.zeros((8, 128), f32)] + direction
                z = [(z[i] if i < len(z) else 0.0) - step * (grown[i] - shifted[i]) for i in range(len(grown))]
                inner_next = inner(z, z, mu)
                ratio = inner_next / inner_now
                direction = [z[i] + ratio * direction[i] if i < len(direction) else z[i] for i in range(len(z))]
                inner_now = inner_next
        return x

    def update(n_step, s):
        w = [coef[n_step, group_of[s], i, s:s + 1, :].reshape(1, 1, 128) for i in range(3)]
        flag = jnp.where(tm - 2 * s == 0, f32(1.0), f32(0.0))
        begin = 3 if n_step == 0 else OWN
        for r, n in blocks(begin, n_step == 0):
            here = (s, slice(begin, WIDE), slice(r, r + n))
            value = w[0] * v0s[here] + w[1] * v1s[here] + w[2] * v2s[here]
            if n_step == 0:
                xs[here] = value + flag * u0[begin:WIDE, r:r + n, :]
            else:
                xs[here] = jnp.where(tm - 2 * s >= 0, value + xs[here], f32(0.0))

    def solve(n_step, g, group):
        for s in group:
            krylov(n_step, s, (1, 4)[n_step])
        if group:
            sum_start(n_step, g)

    def turn_late(n_step):
        if late:
            sum_turn(n_step, 1)

    mom[...] = jnp.zeros(mom.shape, f32)
    solve(0, 0, early)
    solve(0, 1, late)
    sum_turn(0, 0)
    sources(1, 4)
    turn_late(0)
    sum_finish(0, 0)
    for s in early:
        update(0, s)
    solve(1, 0, early)
    if late:
        sum_finish(0, 1)
    for s in late:
        update(0, s)
    solve(1, 1, late)
    sum_turn(1, 0)
    turn_late(1)
    sum_finish(1, 0)
    for s in early:
        update(1, s)

    plan_rows = []
    span = slots // 2
    while span >= 1:
        for s in range(2 * span - 1, span - 1, -1):
            plan_rows.append((s, s - span, 2 * span))
        span //= 2
    plan_rows.append((slots, 0, 1))
    order = [row[0] for row in plan_rows]
    last = len(plan_rows) - 1
    finished = {s: max((p for p, row in enumerate(plan_rows) if row[1] == s), default=-1) for s in order[:-1]}

    def pick(p, values):
        out = values[-1]
        for i in range(len(values) - 2, -1, -1):
            out = jnp.where(p == i, values[i], out)
        return out

    halves = ((LOW, MID), (MID, HIGH))

    def shift(h):
        rows = pl.ds(halves[h][0], NYL // 2)
        return pltpu.make_async_remote_copy(
            src_ref=xs.at[0, pl.ds(OWN, HALF), rows, :], dst_ref=xs.at[slots, pl.ds(OWN, HALF), rows, :],
            send_sem=shift_send.at[h], recv_sem=shift_recv.at[h],
            device_id={"tm": lax.rem(tm + 1, slices)}, device_id_type=MESH,
        )

    def shift_start(h):
        @pl.when(tm < slices - 1)
        def _():
            shift(h).start()

    def pass_on():
        state = xs.at[slots]

        @pl.when(tm == 0)
        def _():
            xs[slots, OWN:WIDE, LOW:HIGH, :] = jnp.zeros((HALF, NYL, 128), f32)

        for h, parts, side in ((0, (0,), -1), (1, (1, 2), 1)):
            @pl.when(tm > 0)
            def _():
                shift(h).wait_recv()

            parts_start(2 + last, state, parts, (side,))

        @pl.when(tm < slices - 1)
        def _():
            for h in range(2):
                shift(h).wait_send()

    waiting = [s for s in order[:-1] if finished[s] < 0]
    if waiting:
        parts_start(2 + order.index(waiting[0]), xs.at[waiting[0]], (0, 1, 2), (-1, 1))
    for s in waiting[1:]:
        parts_start(2 + order.index(s), xs.at[s], (0, 1, 2), (-1, 1))
    if late:
        sum_finish(1, 1)
        for s in late:
            update(1, s)
    if last == 0:
        shift_start(0)
        shift_start(1)
        pass_on()

    def combine(before, now, first, r, n):
        mid, total = beside(now, first, r, n)
        return mid, cg[first:WIDE, r:r + n, :] * mid - ca[first:WIDE, r:r + n, :] * total, before[first:WIDE, r:r + n, :] if before is not None else None

    def section(p, carry):
        at, to = pick(p, order), pick(p, [row[1] for row in plan_rows])
        factor = pick(p, [jnp.float32(2.0 * row[2] / (12.0 * slices)) for row in plan_rows])
        for r, n in chunks(LOW - 8, HIGH + 8, CHUNK):
            a = inv[:, r:r + n, :] * factor
            ca[:, r:r + n, :] = a
            cg[:, r:r + n, :] = 6.0 * a - 2.0
        ts[0][OWN:WIDE, LOW:HIGH, :] = xs[at, OWN:WIDE, LOW:HIGH, :]
        for h, parts, side, segments, (low, high) in (
            (0, (0, 1), 1, ((0, 8), (8, NYL // 2 + 8)), (LOW - 8, MID + 8)),
            (1, (2,), -1, ((16 + NYL // 2, NYL // 2 - 8), (8 + NYL, 8)), (MID, HIGH + 8)),
        ):
            parts_wait(2 + p, xs.at[at], parts, side)
            halo_build(2 + p, ts[0], segments)
            for j in range(1, TERMS - 1):
                for r, n in chunks(low, high, CHUNK):
                    mid, value, before = combine(ts[j - 2] if j > 1 else None, ts[j - 1], j, r, n)
                    ts[j][j:WIDE, r:r + n, :] = 0.5 * value if j == 1 else value - before
            for r, n in chunks(*halves[h], CHUNK):
                mid, value, before = combine(ts[5], ts[6], OWN, r, n)
                value = f32(cheb[7]) * (value - before) + f32(cheb[6]) * mid + f32(cheb[5]) * before
                for j in range(5):
                    value = value + f32(cheb[j]) * ts[j][OWN:WIDE, r:r + n, :]
                xs[to, OWN:WIDE, r:r + n, :] = xs[to, OWN:WIDE, r:r + n, :] + value
            if last > 0:
                @pl.when(p == last - 1)
                def _():
                    shift_start(h)
        for s, p_done in finished.items():
            if p_done >= 0:
                @pl.when(p == p_done)
                def _():
                    parts_start(2 + order.index(s), xs.at[s], (0, 1, 2), (-1, 1))
        if last > 0:
            @pl.when(p == last - 1)
            def _():
                pass_on()
        return carry

    lax.fori_loop(0, last + 1, section, 0)

    for q in range(HALF):
        turned = xs[0, OWN + q, LOW:HIGH, :].T
        nat[1, pl.ds(q, NZ, stride=NXL), :] = turned[0:NZ, :]
        nat[1, pl.ds(NXL - 1 - q, NZ, stride=NXL), :] = turned[NZ:2 * NZ, :]
    store_out = pltpu.make_async_copy(nat.at[1], out_ref, load_sem.at[2])
    store_out.start()

    for n, (a, b) in enumerate(around):
        @pl.when(has(a, b))
        def _():
            pltpu.make_async_remote_copy(
                src_ref=bore_ref, dst_ref=bext.at[1 - b, pl.ds(8 * (1 - a), 8), :],
                send_sem=bore_send.at[n], recv_sem=bore_recv.at[n],
                device_id={"gx": gx + a, "gy": gy + b}, device_id_type=MESH,
            ).wait_send()
            halo_copy(0, heat, n, a, b).wait_send()
            halo_copy(1, u0, n, a, b).wait_send()
            for p, s in enumerate(order):
                if b == 0:
                    for q in range(len(PARTS)):
                        halo_copy(2 + p, xs.at[s], n, a, b, q).wait_send()
                else:
                    halo_copy(2 + p, xs.at[s], n, a, b).wait_send()
    for s in range(1, slots):
        @pl.when(tm + 2 * s < slices)
        def _():
            pltpu.make_async_remote_copy(
                src_ref=plans.at[0], dst_ref=plans.at[s],
                send_sem=plan_send.at[s], recv_sem=plan_recv.at[s],
                device_id={"tm": tm + 2 * s}, device_id_type=MESH,
            ).wait_send()
    store_out.wait()


def per_device(sizes, initial, capacity, profile, bore_loop, plan):
    slices = sizes[0]
    slots = max(1, slices // 2)
    exchanges = 2 + (slots - 1) + 1
    wide = (WIDE, ROWS, 128)
    f32 = jnp.float32
    dma = pltpu.SemaphoreType.DMA
    out = pl.pallas_call(
        functools.partial(kernel, sizes),
        out_shape=jax.ShapeDtypeStruct((NZ * NXL, NYL), f32),
        in_specs=[
            pl.BlockSpec(memory_space=pl.ANY),
            pl.BlockSpec(memory_space=pl.ANY),
            pl.BlockSpec(memory_space=pltpu.VMEM),
            pl.BlockSpec(memory_space=pltpu.VMEM),
            pl.BlockSpec(memory_space=pltpu.VMEM),
        ],
        out_specs=pl.BlockSpec(memory_space=pl.ANY),
        scratch_shapes=[
            pltpu.VMEM((2, NZ * NXL, NYL), f32),
            pltpu.VMEM((STEPS, WIDE, slots * (NYL + 16), 128), f32),
            pltpu.VMEM((exchanges, 2, HALF, NYL + 16, 128), f32),
            pltpu.VMEM((exchanges, 2, HALF, 8, 128), f32),
            pltpu.VMEM((3, 24, 128), jnp.int32),
            pltpu.VMEM((slots, 8, 128), jnp.int32),
            pltpu.VMEM((slots * (NYL + 16), 128), f32),
            pltpu.VMEM((STEPS, 2, 6, 8, 128), f32),
            pltpu.VMEM((STEPS, 2, 2, 8, 128), f32),
            pltpu.VMEM((STEPS, 2, 3, 8, 128), f32),
            pltpu.VMEM((STEPS, 2, 8, 8, 128), f32),
            pltpu.VMEM((STEPS, 2, 8, 8, 128), f32),
            dma((3,)),
            dma((8,)),
            dma((8,)),
            dma((slots,)),
            dma((slots,)),
            dma((exchanges, 8)),
            dma((exchanges, 8)),
            dma((STEPS, 2, 2, 8)),
            dma((STEPS, 2, 2, 8)),
            dma((2,)),
            dma((2,)),
            dma((exchanges, len(PARTS), 8)),
            dma((exchanges, len(PARTS), 8)),
        ] + [pltpu.VMEM(wide, f32)] * 7 + [pltpu.VMEM((slots + 1, *wide), f32)]
        + [pltpu.VMEM((slots, *wide), f32)] * 3 + [pltpu.VMEM(wide, f32)] * (TERMS - 1),
        compiler_params=pltpu.CompilerParams(
            collective_id=0, has_side_effects=True, vmem_limit_bytes=56 * 1024 * 1024
        ),
    )(
        initial.reshape(NZ * NXL, NYL),
        capacity.reshape(NZ * NXL, NYL),
        profile.reshape(1, NZ),
        bore_loop,
        plan[0],
    )
    return out.reshape(1, NZ, NXL, NYL)


def solution(mesh):
    sizes = (mesh.shape["tm"], mesh.shape["gx"], mesh.shape["gy"])
    return jax.shard_map(
        functools.partial(per_device, sizes),
        mesh=mesh,
        in_specs=(
            P(None, "gx", "gy"),
            P(None, "gx", "gy"),
            P(),
            P("gx", "gy"),
            P("tm", None, None),
        ),
        out_specs=P("tm", None, "gx", "gy"),
        check_vma=False,
    )
```

```python
import functools

import jax
import jax.numpy as jnp
import numpy as np
from jax import lax
from jax.experimental import pallas as pl
from jax.experimental.pallas import tpu as pltpu
from jax.sharding import PartitionSpec as P

MESH = pl.DeviceIdType.MESH
STEPS = 2
TERMS = 8
LOOPS = 16
HORIZON = 4.0 / 3.0
EXPONENT = 16.0

NZ, NXL, NYL = 64, 8, 128
HALF = NXL // 2
REACH = TERMS - 1
OWN = REACH
WIDE = REACH + HALF
LAST = WIDE - 1
ROWS = NYL + 32
LOW, HIGH = 16, 16 + NYL
CHUNK = 16
MID = LOW + NYL // 2
PARTS = ((LOW, NYL // 2), (MID, 8), (MID + 8, NYL // 2 - 8))


def cheb_coeffs(term_count):
    angles = np.pi * (np.arange(term_count) + 0.5) / term_count
    cheb_nodes = np.cos(angles)
    samples = np.exp(-EXPONENT * (cheb_nodes + 1.0))
    coeffs = [
        2.0 / term_count * float(np.sum(samples * np.cos(term_index * angles)))
        for term_index in range(term_count)
    ]
    coeffs[0] = coeffs[0] / 2.0
    return coeffs


def chunks(low, high, size):
    return [(r, min(size, high - r)) for r in range(low, high, size)]


def kernel(
    sizes,
    init_hbm, cap_hbm, prof_ref, bore_ref, plan_ref, out_ref,
    nat, src, xbuf, hbuf, bext, plans, rates, mom, pay, coef, sums_x, sums_y,
    load_sem, bore_send, bore_recv, plan_send, plan_recv, halo_send, halo_recv,
    sum_send, sum_recv, shift_send, shift_recv, part_send, part_recv,
    heat, inv, dinv, u0, ku, ca, cg, xs, v0s, v1s, v2s, *ts,
):
    slices, nx, ny = sizes
    slots = max(1, slices // 2)
    inv_step = STEPS * slices / HORIZON
    tm, gx, gy = lax.axis_index("tm"), lax.axis_index("gx"), lax.axis_index("gy")
    f32 = jnp.float32
    cheb = cheb_coeffs(TERMS)

    def has(a, b):
        x, y = gx + a, gy + b
        return (x >= 0) & (x < nx) & (y >= 0) & (y < ny)

    around = [(a, b) for b in (-1, 0, 1) for a in (-1, 0, 1) if (a, b) != (0, 0)]
    around.sort(key=lambda ab: ab[1] == 0)

    load_cap = pltpu.make_async_copy(cap_hbm, nat.at[0], load_sem.at[0])
    load_init = pltpu.make_async_copy(init_hbm, nat.at[1], load_sem.at[1])
    load_cap.start()
    load_init.start()

    barrier = pltpu.get_barrier_semaphore()
    for d in range(1, nx):
        pl.semaphore_signal(barrier, inc=1, device_id={"gx": lax.rem(gx + d, nx)}, device_id_type=MESH)
    for d in range(1, ny):
        pl.semaphore_signal(barrier, inc=1, device_id={"gy": lax.rem(gy + d, ny)}, device_id_type=MESH)
    for a, b in around:
        if a and b:
            @pl.when(has(a, b))
            def _():
                pl.semaphore_signal(barrier, inc=1, device_id={"gx": gx + a, "gy": gy + b}, device_id_type=MESH)
    spans = [1] + [2 * s for s in range(1, slots)]
    for s in spans:
        @pl.when(tm >= s)
        def _():
            pl.semaphore_signal(barrier, inc=1, device_id={"tm": tm - s}, device_id_type=MESH)

    lane = lax.broadcasted_iota(jnp.int32, (8, 128), 1)

    def halo_copy(e, at, n, a, b, q=None):
        first, size = (LOW, NYL) if q is None else PARTS[q]
        rows = pl.ds(first, size) if b == 0 else pl.ds(LOW, 8) if b < 0 else pl.ds(HIGH - 8, 8)
        if a == 0:
            dst = hbuf.at[e, 1 if b < 0 else 0]
        else:
            at_rows = pl.ds(first - LOW + 8, size) if b == 0 else pl.ds(8 + NYL, 8) if b < 0 else pl.ds(0, 8)
            dst = xbuf.at[e, 1 if a < 0 else 0, :, at_rows, :]
        return pltpu.make_async_remote_copy(
            src_ref=at.at[pl.ds(OWN, HALF), rows, :], dst_ref=dst,
            send_sem=halo_send.at[e, n] if q is None else part_send.at[e, q, n],
            recv_sem=halo_recv.at[e, n] if q is None else part_recv.at[e, q, n],
            device_id={"gx": gx + a, "gy": gy + b}, device_id_type=MESH,
        )

    def parts_start(e, at, parts, sides):
        for n, (a, b) in enumerate(around):
            if b in sides:
                @pl.when(has(a, b))
                def _():
                    halo_copy(e, at, n, a, b).start()
        for q in parts:
            for n, (a, b) in enumerate(around):
                if b == 0:
                    @pl.when(has(a, b))
                    def _():
                        halo_copy(e, at, n, a, b, q).start()

    def parts_wait(e, at, parts, side):
        for n, (a, b) in enumerate(around):
            if b == side or b == 0:
                @pl.when(has(-a, -b))
                def _():
                    if b == 0:
                        for q in parts:
                            halo_copy(e, at, n, a, b, q).wait_recv()
                    else:
                        halo_copy(e, at, n, a, b).wait_recv()

    def halo_start(e, at):
        for n, (a, b) in sorted(enumerate(around), key=lambda item: item[1][1] != 0):
            @pl.when(has(a, b))
            def _():
                halo_copy(e, at, n, a, b).start()

    def halo_wait(e, at):
        for n, (a, b) in enumerate(around):
            @pl.when(has(-a, -b))
            def _():
                halo_copy(e, at, n, a, b).wait_recv()

    left, right, down, up = gx > 0, gx < nx - 1, gy > 0, gy < ny - 1

    low_lanes = lax.broadcasted_iota(jnp.int32, (1, 8, 128), 2) < NZ

    def halo_build(e, at, segments=((0, 8), (8, NYL), (8 + NYL, 8))):
        for r, n in segments:
            edge = down if r == 0 else up if r == 8 + NYL else True
            for crossed in (False, True):
                from_left = (~low_lanes if crossed else low_lanes) & left & edge
                from_right = (low_lanes if crossed else ~low_lanes) & right & edge
                for m in range(HALF - 1, REACH) if crossed else range(HALF - 1):
                    q = REACH - 1 - m if crossed else m + 1
                    one = xbuf[e, 0, q, r:r + n, :].reshape(n // 8, 8, 128)
                    two = xbuf[e, 1, q, r:r + n, :].reshape(n // 8, 8, 128)
                    value = jnp.where(from_left, one, jnp.where(from_right, two, f32(0.0)))
                    if crossed:
                        value = pltpu.roll(value, NZ, 2)
                    at[m, LOW - 8 + r:LOW - 8 + r + n, :] = value.reshape(n, 128)
        if (0, 8) in segments:
            at[OWN:WIDE, LOW - 8:LOW, :] = jnp.where(down, hbuf[e, 0], f32(0.0))
        if (8 + NYL, 8) in segments:
            at[OWN:WIDE, HIGH:HIGH + 8, :] = jnp.where(up, hbuf[e, 1], f32(0.0))

    def to_wide(which, at):
        for q in range(HALF):
            top = nat[which, pl.ds(q, NZ, stride=NXL), :]
            low = nat[which, pl.ds(NXL - 1 - q, NZ, stride=NXL), :]
            at[OWN + q, LOW:HIGH, :] = jnp.concatenate([top, low], axis=0).T

    greeted = nx - 1 + ny - 1
    for a, b in around:
        if a and b:
            greeted = greeted + jnp.where(has(a, b), 1, 0)
    for s in spans:
        greeted = greeted + jnp.where(tm + s < slices, 1, 0)
    pl.semaphore_wait(barrier, greeted)
    plans[0] = jnp.zeros((8, 128), jnp.int32)
    plans[0, 0:STEPS, 0:LOOPS] = plan_ref[...]
    bext[1, 8:16, :] = bore_ref[...]
    for n, (a, b) in enumerate(around):
        @pl.when(has(a, b))
        def _():
            pltpu.make_async_remote_copy(
                src_ref=bore_ref, dst_ref=bext.at[1 - b, pl.ds(8 * (1 - a), 8), :],
                send_sem=bore_send.at[n], recv_sem=bore_recv.at[n],
                device_id={"gx": gx + a, "gy": gy + b}, device_id_type=MESH,
            ).start()
    for s in range(1, slots):
        @pl.when(tm + 2 * s < slices)
        def _():
            pltpu.make_async_remote_copy(
                src_ref=plans.at[0], dst_ref=plans.at[s],
                send_sem=plan_send.at[s], recv_sem=plan_recv.at[s],
                device_id={"tm": tm + 2 * s}, device_id_type=MESH,
            ).start()

    load_cap.wait()
    to_wide(0, heat)
    halo_start(0, heat)
    load_init.wait()
    to_wide(1, u0)
    halo_start(1, u0)

    for sy in range(3):
        for sx in range(3):
            if (sx, sy) != (1, 1):
                @pl.when(~has(sx - 1, sy - 1))
                def _():
                    bext[sy, 8 * sx:8 * sx + 8, :] = jnp.full((8, 128), LOOPS, jnp.int32)
    for n, (a, b) in enumerate(around):
        @pl.when(has(-a, -b))
        def _():
            pltpu.make_async_remote_copy(
                src_ref=bore_ref, dst_ref=bext.at[1 - b, pl.ds(8 * (1 - a), 8), :],
                send_sem=bore_send.at[n], recv_sem=bore_recv.at[n],
                device_id={"gx": gx - a, "gy": gy - b}, device_id_type=MESH,
            ).wait_recv()
    for s in range(1, slots):
        @pl.when(tm - 2 * s >= 0)
        def _():
            pltpu.make_async_remote_copy(
                src_ref=plans.at[0], dst_ref=plans.at[s],
                send_sem=plan_send.at[s], recv_sem=plan_recv.at[s],
                device_id={"tm": tm - 2 * s}, device_id_type=MESH,
            ).wait_recv()

        @pl.when(tm - 2 * s < 0)
        def _():
            plans[s] = plans[0]

    SPAN = NYL + 16
    loops = jnp.concatenate([bext[0], bext[1], bext[2]], axis=0)
    depth = jnp.concatenate([prof_ref[...], prof_ref[...]], axis=1)

    def sources(n_step, first):
        for s in range(slots):
            table = plans[s].astype(f32) - 3.5
            rate = jnp.zeros((72, 128), f32)
            for v in range(LOOPS):
                rate = jnp.where(loops == v, jnp.broadcast_to(table[n_step:n_step + 1, v:v + 1], (72, 128)), rate)
            turned = jnp.concatenate([rate, jnp.zeros((56, 128), f32)], axis=0).T
            at_row = s * SPAN
            rates[at_row:at_row + 8, :] = pltpu.roll(turned[120:128, :], 24, 1)
            rates[at_row + 8:at_row + 8 + NYL, :] = turned
            rates[at_row + 8 + NYL:at_row + SPAN, :] = pltpu.roll(turned[0:8, :], 104, 1)
        all_rates = rates[...].astype(jnp.bfloat16)

        def spread(m, carry):
            here = 32 + m - REACH
            there = 32 + NXL - 1 - (m - REACH)
            pick_row = lax.broadcasted_iota(jnp.int32, (128, 128), 0)
            pick_lane = lax.broadcasted_iota(jnp.int32, (128, 128), 1)
            pick = jnp.where(pick_row == jnp.where(pick_lane < NZ, here, there), f32(1.0), f32(0.0)).astype(jnp.bfloat16)
            wide = jnp.dot(all_rates, pick, preferred_element_type=f32)
            src[n_step, m] = wide * depth
            return carry

        lax.fori_loop(first, WIDE, spread, 0)

    sources(0, 1)

    def rolled(value, by):
        return pltpu.roll(value, by, 2)

    def beside(at, first, r, n):
        count = WIDE - first
        mid = at[first:WIDE, r:r + n, :]
        before = jnp.concatenate([at[first - 1:first, r:r + n, :], mid[:-1]], axis=0) if count > 1 else at[first - 1:first, r:r + n, :]
        across = rolled(mid[-1:], NZ)
        after = jnp.concatenate([mid[1:], across], axis=0) if count > 1 else across
        cols = at[first:WIDE, r - 1:r - 1 + n, :] + at[first:WIDE, r + 1:r + 1 + n, :]
        z_lane = lax.broadcasted_iota(jnp.int32, (count, n, 128), 2) & (NZ - 1)
        above = jnp.where(z_lane != 0, rolled(mid, 1), f32(0.0))
        below = jnp.where(z_lane != NZ - 1, rolled(mid, 127), f32(0.0))
        return mid, ((before + after) + cols) + (above + below)

    def blocks(first, wide):
        return chunks(LOW - 8, HIGH + 8, CHUNK) if wide else chunks(LOW, HIGH, CHUNK)

    def add_own(total, value, first, r, n):
        value = value[OWN - first:]
        low, high = max(LOW - r, 0), min(HIGH - r, n)
        if high <= low:
            return total
        value = value[:, low:high, :]
        return total + jnp.sum(value.reshape(-1, 8, 128), axis=0)

    halo_wait(0, heat)
    halo_build(0, heat)

    for r, n in chunks(LOW - 8, HIGH + 8, CHUNK):
        cap = heat[:, r:r + n, :]
        inside = cap > 0.0
        dinv[:, r:r + n, :] = jnp.where(inside, 1.0 / (cap * f32(inv_step) + 6.0), f32(0.0))
        inv[:, r:r + n, :] = jnp.where(inside, 1.0 / cap, f32(0.0))

    halo_wait(1, u0)
    halo_build(1, u0)
    for r, n in blocks(1, True):
        mid, total = beside(u0, 1, r, n)
        ku[1:WIDE, r:r + n, :] = 6.0 * mid - total

    zero = jnp.zeros((8, 128), f32)
    early, late = list(range(slots - 1, slots // 2 - 1, -1)), list(range(slots // 2 - 1, -1, -1))
    group_of = {s: g for g, group in enumerate((early, late)) for s in group}

    def krylov(n_step, s, first):
        x, v0, v1, v2 = xs.at[s], v0s.at[s], v1s.at[s], v2s.at[s]
        flag = jnp.where(tm - 2 * s == 0, f32(1.0), f32(0.0))
        base = s * SPAN
        sums = [zero] * 6
        for r, n in blocks(first, True):
            residual = src[n_step, first:WIDE, base + (r - 8):base + (r - 8) + n, :]
            if n_step == 0:
                residual = residual - flag * ku[first:WIDE, r:r + n, :]
            else:
                mid, total = beside(x, first, r, n)
                residual = residual - (6.0 * mid - total)
            z = dinv[first:WIDE, r:r + n, :] * residual
            v0[first:WIDE, r:r + n, :] = z
            sums[0] = add_own(sums[0], residual * z, first, r, n)
        for k, (now, then) in enumerate(((v0, v1), (v1, v2))):
            begin = first + 1 + k
            for r, n in blocks(begin, True):
                mid, total = beside(now, begin, r, n)
                z = dinv[begin:WIDE, r:r + n, :] * total
                then[begin:WIDE, r:r + n, :] = z
                sums[2 * k + 1] = add_own(sums[2 * k + 1], mid * total, begin, r, n)
                sums[2 * k + 2] = add_own(sums[2 * k + 2], z * total, begin, r, n)
        for r, n in blocks(OWN, False):
            mid, total = beside(v2, OWN, r, n)
            sums[5] = add_own(sums[5], mid * total, OWN, r, n)
        for j, total in enumerate(sums):
            mom[n_step, group_of[s], j, s:s + 1, :] = jnp.sum(total, axis=0, keepdims=True)

    stages = (("gx", nx, gx, sums_x), ("gy", ny, gy, sums_y))

    def sum_copy(n_step, g, stage, d):
        axis, count, me, buf = stages[stage]
        return pltpu.make_async_remote_copy(
            src_ref=pay.at[n_step, g, stage], dst_ref=buf.at[n_step, g, d],
            send_sem=sum_send.at[n_step, g, stage, d], recv_sem=sum_recv.at[n_step, g, stage, d],
            device_id={axis: lax.rem(me + d, count)}, device_id_type=MESH,
        )

    def sum_send_all(n_step, g, stage):
        for d in range(1, stages[stage][1]):
            sum_copy(n_step, g, stage, d).start()

    def sum_collect(n_step, g, stage):
        for d in range(1, stages[stage][1]):
            sum_copy(n_step, g, stage, d).wait_recv()
        total = pay[n_step, g, stage]
        for d in range(1, stages[stage][1]):
            total = total + stages[stage][3][n_step, g, d]
        return total

    def sum_start(n_step, g):
        packed = jnp.zeros((8, 128), f32)
        for j in range(6):
            packed = jnp.where(lane == j, jnp.sum(mom[n_step, g, j], axis=1, keepdims=True), packed)
        pay[n_step, g, 0] = packed
        sum_send_all(n_step, g, 0)

    def sum_turn(n_step, g):
        pay[n_step, g, 1] = sum_collect(n_step, g, 0)
        sum_send_all(n_step, g, 1)

    def sum_finish(n_step, g):
        total = sum_collect(n_step, g, 1)
        weights = cg_coefficients([jnp.broadcast_to(total[:, j:j + 1], (8, 128)) for j in range(6)])
        for i in range(3):
            coef[n_step, g, i] = weights[i]

    def sum_drain():
        for n_step in range(STEPS):
            for g in range(2 if late else 1):
                for stage in range(2):
                    for d in range(1, stages[stage][1]):
                        sum_copy(n_step, g, stage, d).wait_send()

    def cg_coefficients(mu):
        def inner(p, q, m):
            total = None
            for i, a in enumerate(p):
                for j, b in enumerate(q):
                    term = a * b * m[i + j]
                    total = term if total is None else total + term
            return total

        gap = [mu[j] - mu[j + 1] for j in range(5)]
        one = jnp.ones((8, 128), f32)
        x = [jnp.zeros((8, 128), f32)] * 3
        z, direction = [one], [one]
        inner_now = mu[0]
        for it in range(3):
            step = inner_now / inner(direction, direction, gap)
            x = [x[i] + step * direction[i] if i < len(direction) else x[i] for i in range(3)]
            if it < 2:
                grown = direction + [jnp.zeros((8, 128), f32)]
                shifted = [jnp.zeros((8, 128), f32)] + direction
                z = [(z[i] if i < len(z) else 0.0) - step * (grown[i] - shifted[i]) for i in range(len(grown))]
                inner_next = inner(z, z, mu)
                ratio = inner_next / inner_now
                direction = [z[i] + ratio * direction[i] if i < len(direction) else z[i] for i in range(len(z))]
                inner_now = inner_next
        return x

    def update(n_step, s):
        w = [coef[n_step, group_of[s], i, s:s + 1, :].reshape(1, 1, 128) for i in range(3)]
        flag = jnp.where(tm - 2 * s == 0, f32(1.0), f32(0.0))
        begin = 3 if n_step == 0 else OWN
        for r, n in blocks(begin, n_step == 0):
            here = (s, slice(begin, WIDE), slice(r, r + n))
            value = w[0] * v0s[here] + w[1] * v1s[here] + w[2] * v2s[here]
            if n_step == 0:
                xs[here] = value + flag * u0[begin:WIDE, r:r + n, :]
            else:
                xs[here] = jnp.where(tm - 2 * s >= 0, value + xs[here], f32(0.0))

    def solve(n_step, g, group):
        for s in group:
            krylov(n_step, s, (1, 4)[n_step])
        if group:
            sum_start(n_step, g)

    def turn_late(n_step):
        if late:
            sum_turn(n_step, 1)

    mom[...] = jnp.zeros(mom.shape, f32)
    solve(0, 0, early)
    solve(0, 1, late)
    sum_turn(0, 0)
    sources(1, 4)
    turn_late(0)
    sum_finish(0, 0)
    for s in early:
        update(0, s)
    solve(1, 0, early)
    if late:
        sum_finish(0, 1)
    for s in late:
        update(0, s)
    solve(1, 1, late)
    sum_turn(1, 0)
    turn_late(1)
    sum_finish(1, 0)
    for s in early:
        update(1, s)

    plan_rows = []
    span = slots // 2
    while span >= 1:
        for s in range(2 * span - 1, span - 1, -1):
            plan_rows.append((s, s - span, 2 * span))
        span //= 2
    plan_rows.append((slots, 0, 1))
    order = [row[0] for row in plan_rows]
    last = len(plan_rows) - 1
    finished = {s: max((p for p, row in enumerate(plan_rows) if row[1] == s), default=-1) for s in order[:-1]}

    def pick(p, values):
        out = values[-1]
        for i in range(len(values) - 2, -1, -1):
            out = jnp.where(p == i, values[i], out)
        return out

    halves = ((LOW, MID), (MID, HIGH))

    def shift(h):
        rows = pl.ds(halves[h][0], NYL // 2)
        return pltpu.make_async_remote_copy(
            src_ref=xs.at[0, pl.ds(OWN, HALF), rows, :], dst_ref=xs.at[slots, pl.ds(OWN, HALF), rows, :],
            send_sem=shift_send.at[h], recv_sem=shift_recv.at[h],
            device_id={"tm": lax.rem(tm + 1, slices)}, device_id_type=MESH,
        )

    def shift_start(h):
        @pl.when(tm < slices - 1)
        def _():
            shift(h).start()

    def pass_on():
        state = xs.at[slots]

        @pl.when(tm == 0)
        def _():
            xs[slots, OWN:WIDE, LOW:HIGH, :] = jnp.zeros((HALF, NYL, 128), f32)

        sum_drain()
        for h, parts, side in ((0, (0,), -1), (1, (1, 2), 1)):
            @pl.when(tm > 0)
            def _():
                shift(h).wait_recv()

            parts_start(2 + last, state, parts, (side,))

        @pl.when(tm < slices - 1)
        def _():
            for h in range(2):
                shift(h).wait_send()

    waiting = [s for s in order[:-1] if finished[s] < 0]
    if waiting:
        parts_start(2 + order.index(waiting[0]), xs.at[waiting[0]], (0, 1, 2), (-1, 1))
    for s in waiting[1:]:
        parts_start(2 + order.index(s), xs.at[s], (0, 1, 2), (-1, 1))
    if late:
        sum_finish(1, 1)
        for s in late:
            update(1, s)
    if last == 0:
        shift_start(0)
        shift_start(1)
        pass_on()

    def combine(before, now, first, r, n):
        mid, total = beside(now, first, r, n)
        return mid, cg[first:WIDE, r:r + n, :] * mid - ca[first:WIDE, r:r + n, :] * total, before[first:WIDE, r:r + n, :] if before is not None else None

    def section(p, carry):
        at, to = pick(p, order), pick(p, [row[1] for row in plan_rows])
        factor = pick(p, [jnp.float32(2.0 * row[2] / (12.0 * slices)) for row in plan_rows])
        fresh = pick(p, [i == 0 or row[2] != plan_rows[i - 1][2] for i, row in enumerate(plan_rows)])

        @pl.when(fresh)
        def _():
            for r, n in chunks(LOW - 8, HIGH + 8, CHUNK):
                a = inv[:, r:r + n, :] * factor
                ca[:, r:r + n, :] = a
                cg[:, r:r + n, :] = 6.0 * a - 2.0

        ts[0][OWN:WIDE, LOW:HIGH, :] = xs[at, OWN:WIDE, LOW:HIGH, :]
        for h, parts, side, segments, (low, high) in (
            (0, (0, 1), 1, ((0, 8), (8, NYL // 2 + 8)), (LOW - 8, MID + 8)),
            (1, (2,), -1, ((16 + NYL // 2, NYL // 2 - 8), (8 + NYL, 8)), (MID, HIGH + 8)),
        ):
            parts_wait(2 + p, xs.at[at], parts, side)
            halo_build(2 + p, ts[0], segments)
            for j in range(1, TERMS - 1):
                for r, n in chunks(low, high, CHUNK):
                    mid, value, before = combine(ts[j - 2] if j > 1 else None, ts[j - 1], j, r, n)
                    ts[j][j:WIDE, r:r + n, :] = 0.5 * value if j == 1 else value - before
            for r, n in chunks(*halves[h], CHUNK):
                mid, value, before = combine(ts[5], ts[6], OWN, r, n)
                value = f32(cheb[7]) * (value - before) + f32(cheb[6]) * mid + f32(cheb[5]) * before
                for j in range(5):
                    value = value + f32(cheb[j]) * ts[j][OWN:WIDE, r:r + n, :]
                xs[to, OWN:WIDE, r:r + n, :] = xs[to, OWN:WIDE, r:r + n, :] + value
            for s, p_done in finished.items():
                if p_done >= 0:
                    @pl.when(p == p_done)
                    def _():
                        parts_start(2 + order.index(s), xs.at[s], ((0,), (1, 2))[h], ((-1,), (1,))[h])
            if last > 0:
                @pl.when(p == last - 1)
                def _():
                    shift_start(h)
        if last > 0:
            @pl.when(p == last - 1)
            def _():
                pass_on()
        return carry

    lax.fori_loop(0, last + 1, section, 0)

    for q in range(HALF):
        turned = xs[0, OWN + q, LOW:HIGH, :].T
        nat[1, pl.ds(q, NZ, stride=NXL), :] = turned[0:NZ, :]
        nat[1, pl.ds(NXL - 1 - q, NZ, stride=NXL), :] = turned[NZ:2 * NZ, :]
    store_out = pltpu.make_async_copy(nat.at[1], out_ref, load_sem.at[2])
    store_out.start()

    for n, (a, b) in enumerate(around):
        @pl.when(has(a, b))
        def _():
            pltpu.make_async_remote_copy(
                src_ref=bore_ref, dst_ref=bext.at[1 - b, pl.ds(8 * (1 - a), 8), :],
                send_sem=bore_send.at[n], recv_sem=bore_recv.at[n],
                device_id={"gx": gx + a, "gy": gy + b}, device_id_type=MESH,
            ).wait_send()
            halo_copy(0, heat, n, a, b).wait_send()
            halo_copy(1, u0, n, a, b).wait_send()
            for p, s in enumerate(order):
                if b == 0:
                    for q in range(len(PARTS)):
                        halo_copy(2 + p, xs.at[s], n, a, b, q).wait_send()
                else:
                    halo_copy(2 + p, xs.at[s], n, a, b).wait_send()
    for s in range(1, slots):
        @pl.when(tm + 2 * s < slices)
        def _():
            pltpu.make_async_remote_copy(
                src_ref=plans.at[0], dst_ref=plans.at[s],
                send_sem=plan_send.at[s], recv_sem=plan_recv.at[s],
                device_id={"tm": tm + 2 * s}, device_id_type=MESH,
            ).wait_send()
    store_out.wait()


def per_device(sizes, initial, capacity, profile, bore_loop, plan):
    slices = sizes[0]
    slots = max(1, slices // 2)
    exchanges = 2 + (slots - 1) + 1
    wide = (WIDE, ROWS, 128)
    f32 = jnp.float32
    dma = pltpu.SemaphoreType.DMA
    out = pl.pallas_call(
        functools.partial(kernel, sizes),
        out_shape=jax.ShapeDtypeStruct((NZ * NXL, NYL), f32),
        in_specs=[
            pl.BlockSpec(memory_space=pl.ANY),
            pl.BlockSpec(memory_space=pl.ANY),
            pl.BlockSpec(memory_space=pltpu.VMEM),
            pl.BlockSpec(memory_space=pltpu.VMEM),
            pl.BlockSpec(memory_space=pltpu.VMEM),
        ],
        out_specs=pl.BlockSpec(memory_space=pl.ANY),
        scratch_shapes=[
            pltpu.VMEM((2, NZ * NXL, NYL), f32),
            pltpu.VMEM((STEPS, WIDE, slots * (NYL + 16), 128), f32),
            pltpu.VMEM((exchanges, 2, HALF, NYL + 16, 128), f32),
            pltpu.VMEM((exchanges, 2, HALF, 8, 128), f32),
            pltpu.VMEM((3, 24, 128), jnp.int32),
            pltpu.VMEM((slots, 8, 128), jnp.int32),
            pltpu.VMEM((slots * (NYL + 16), 128), f32),
            pltpu.VMEM((STEPS, 2, 6, 8, 128), f32),
            pltpu.VMEM((STEPS, 2, 2, 8, 128), f32),
            pltpu.VMEM((STEPS, 2, 3, 8, 128), f32),
            pltpu.VMEM((STEPS, 2, 8, 8, 128), f32),
            pltpu.VMEM((STEPS, 2, 8, 8, 128), f32),
            dma((3,)),
            dma((8,)),
            dma((8,)),
            dma((slots,)),
            dma((slots,)),
            dma((exchanges, 8)),
            dma((exchanges, 8)),
            dma((STEPS, 2, 2, 8)),
            dma((STEPS, 2, 2, 8)),
            dma((2,)),
            dma((2,)),
            dma((exchanges, len(PARTS), 8)),
            dma((exchanges, len(PARTS), 8)),
        ] + [pltpu.VMEM(wide, f32)] * 7 + [pltpu.VMEM((slots + 1, *wide), f32)]
        + [pltpu.VMEM((slots, *wide), f32)] * 3 + [pltpu.VMEM(wide, f32)] * (TERMS - 1),
        compiler_params=pltpu.CompilerParams(
            collective_id=0, has_side_effects=True, vmem_limit_bytes=56 * 1024 * 1024
        ),
    )(
        initial.reshape(NZ * NXL, NYL),
        capacity.reshape(NZ * NXL, NYL),
        profile.reshape(1, NZ),
        bore_loop,
        plan[0],
    )
    return out.reshape(1, NZ, NXL, NYL)


def solution(mesh):
    sizes = (mesh.shape["tm"], mesh.shape["gx"], mesh.shape["gy"])
    return jax.shard_map(
        functools.partial(per_device, sizes),
        mesh=mesh,
        in_specs=(
            P(None, "gx", "gy"),
            P(None, "gx", "gy"),
            P(),
            P("gx", "gy"),
            P("tm", None, None),
        ),
        out_specs=P("tm", None, "gx", "gy"),
        check_vma=False,
    )
```
